128 devices in a mesh: gen: 8 (over y_hi, x), dom: 8 (over z, y_lo), dp: 2 (over core).
Axes of the slice: x: 4, y: 4 (y_hi: 2, y_lo: 2; y = y_hi * 2 + y_lo), z: 4, core: 2. Of those that a mesh axis runs over, the one named last changes fastest.
Arguments:
- gen_hidden: bfloat16 [2048, 4096], P(('dp', 'dom'), 'gen'), parts along dimension 0, may hold values from -52 to 52
- gen_gain: float32 [8192], P('dp'), parts along dimension 0, may hold values from 0.25 to 1.75
- gen_head: bfloat16 [131072, 4096], P(('dp', 'gen', 'dom')), parts along dimension 0, may hold values from -24 to 24
- dom_hidden: bfloat16 [2048, 4096], P(('dp', 'gen'), 'dom'), parts along dimension 0, may hold values from -52 to 52
- dom_gain: float32 [8192], P('dp'), parts along dimension 0, may hold values from 0.25 to 1.75
- dom_head: bfloat16 [131072, 4096], P(('dp', 'gen', 'dom')), parts along dimension 0, may hold values from -24 to 24
- targets: int32 [2048], P('dp'), parts along dimension 0, may hold values from 0 to 65535
- doc_ids: int32 [2048], P('dp'), parts along dimension 0, may hold values from -1 to 63, as said below
Outputs:
- token_diff: float32 [2048], P(('dp', 'dom')), parts along dimension 0
- doc_score: float32 [128], P(('dp', 'dom')), parts along dimension 0
The draws below stay inside these ranges and needn't reach their ends.
There are 2 independent parts, one for each index of `dp`. The reference program is written for one: setup_inputs(seed, part) draws one part's arguments, and reference() takes and returns one part's arrays. A program takes and returns all parts, laid end to end along the dimension named above; each array names one. Nothing has to cross between parts.
Inputs may be any that keep to these rules, and one draw needn't show every extreme that they name: `doc_ids`: rows 128 * p to 128 * p + 127 form pack p. Each pack begins with rows of exactly 8 documents, numbered 8 * p onwards in order, each one row or more, and ends with padding rows marked -1. The packs fall into pairs whose document rows add up to 136, so the batch holds 544 document rows, and some pack has no padding.
All inputs are finite; a program needn't handle non-finite values.
Results may differ from the reference program's by a relative error of at most 0.0045.
Values may be sent and summed in bfloat16 or wider, within the bound.
A program may use at most 128 MiB of HBM per device.

```python
import math
import jax
import jax.numpy as jnp
import numpy as np
from jax import lax

D = 4096
V = 65536
ROWS_DEV = 128
DOC_PACK = 8
ROWS = 1024
DOCS = 64


def pack_layout(key):
    base = jax.random.fold_in(key, 5)
    key_order, key_length, key_pair, key_side, key_cuts = jax.random.split(base, 5)
    pack_count = ROWS // ROWS_DEV
    half_count = pack_count // 2
    order = jax.random.permutation(key_order, pack_count)
    first_len = jax.random.randint(key_length, (half_count,), DOC_PACK, ROWS_DEV + 1)
    full_pair = jax.random.randint(key_pair, (), 0, half_count)
    side_full = jax.random.randint(key_side, (), 0, 2)
    forced = jnp.where(side_full == 0, ROWS_DEV, DOC_PACK)
    first_len = jnp.where(jnp.arange(half_count) == full_pair, forced, first_len)
    second_len = ROWS_DEV + DOC_PACK - first_len
    both_len = jnp.concatenate([first_len, second_len]).astype(jnp.int32)
    lengths = jnp.zeros((pack_count,), jnp.int32).at[order].set(both_len)
    positions = jnp.arange(ROWS_DEV, dtype=jnp.int32)
    scores = jax.random.randint(key_cuts, (pack_count, ROWS_DEV), 0, 1048576) * ROWS_DEV + positions[None, :]
    usable = (positions[None, :] >= 1) & (positions[None, :] < lengths[:, None])
    scores = jnp.where(usable, scores, -1 - positions[None, :])
    cuts = lax.top_k(scores, DOC_PACK - 1)[1]
    local_doc = jnp.sum((cuts[:, None, :] <= positions[None, :, None]).astype(jnp.int32), axis=2)
    numbered = jnp.arange(pack_count, dtype=jnp.int32)[:, None] * DOC_PACK + local_doc
    doc_table = jnp.where(positions[None, :] < lengths[:, None], numbered, -1)
    return doc_table.reshape(ROWS).astype(jnp.int32)


def model_pair(key, salt_value):
    base = jax.random.fold_in(key, salt_value)
    keys = jax.random.split(base, 4)
    spread = jnp.exp(jax.random.uniform(keys[0], (V, 1), jnp.float32, 0.0, math.log(10.0)))
    trend = 1.0 + 0.2 * jnp.arange(V, dtype=jnp.float32)[:, None] / V
    weights = jax.random.truncated_normal(keys[1], -4.0, 4.0, (V, D), jnp.float32)
    weights = weights * (0.8 * spread * trend / math.sqrt(D))
    hidden = jax.random.truncated_normal(keys[3], -5.0, 5.0, (ROWS, D), jnp.float32)
    return (hidden.astype(jnp.bfloat16), weights.astype(jnp.bfloat16))


def draw_gen_hidden(key, part):
    return model_pair(key, 11)[0]


def draw_gen_head(key, part):
    return model_pair(key, 11)[1]


def draw_dom_hidden(key, part):
    return model_pair(key, 23)[0]


def draw_dom_head(key, part):
    return model_pair(key, 23)[1]


def draw_doc_ids(key, part):
    return pack_layout(key)


def with_ends(values, rng, low, top_value):
    place = [jax.random.randint(jax.random.fold_in(rng, axis), (), 0, length) for axis, length in enumerate(values.shape)]
    longest = values.shape.index(max(values.shape))
    beside = place[:longest] + [(place[longest] + 1) % values.shape[longest]] + place[longest + 1:]
    return values.at[tuple(place)].set(low).at[tuple(beside)].set(top_value)


def rank_bounds(count, lean):
    loads = [(1 << 20) // math.isqrt(standing ** lean) + 1 for standing in range(1, count + 1)]
    scale = 1 + sum(loads) // (1 << 30)
    return np.cumsum(np.array([max(1, weight // scale) for weight in loads]))


def ranked(stream_key, extent, count, lean):
    grid = rank_bounds(count, lean)
    pick = jax.random.randint(jax.random.fold_in(stream_key, 1), extent, 0, int(grid[count - 1]))
    grade = jnp.searchsorted(jnp.asarray(grid, jnp.int32), pick, side="right")
    return jax.random.permutation(jax.random.fold_in(stream_key, 2), count)[grade].astype(jnp.int32)


def setup_inputs(seed: int = 0, part: int = 0) -> dict:
    key_list = jax.random.split(jax.random.key(seed), 9)
    part_keys = jax.random.split(jax.random.fold_in(key_list[8], part), 9)
    return {
        "gen_hidden": draw_gen_hidden(jax.random.fold_in(jax.random.fold_in(key_list[8], part), 71), part),
        "gen_gain": jnp.clip(1.0 + 0.15 * jax.random.normal(part_keys[1], (D,), jnp.float32), 0.25, 1.75),
        "gen_head": draw_gen_head(jax.random.fold_in(jax.random.fold_in(key_list[8], part), 71), part),
        "dom_hidden": draw_dom_hidden(jax.random.fold_in(jax.random.fold_in(key_list[8], part), 71), part),
        "dom_gain": jnp.clip(1.0 + 0.15 * jax.random.normal(part_keys[4], (D,), jnp.float32), 0.25, 1.75),
        "dom_head": draw_dom_head(jax.random.fold_in(jax.random.fold_in(key_list[8], part), 71), part),
        "targets": with_ends(ranked(part_keys[6], (ROWS,), V, 2), jax.random.fold_in(part_keys[6], 3), 0, V - 1).astype(jnp.int32),
        "doc_ids": draw_doc_ids(jax.random.fold_in(jax.random.fold_in(key_list[8], part), 71), part),
    }


def normalize(hidden, scaling):
    values = hidden.astype(jnp.float32)
    meansq = lax.optimization_barrier(jnp.mean(values * values, axis=-1, keepdims=True))
    return (values * lax.rsqrt(meansq + 1e-05) * scaling).astype(jnp.bfloat16)

def log_probs(normed, weights, targets):
    row_blocks = normed.reshape(ROWS // ROWS_DEV, ROWS_DEV, D)
    target_blocks = targets.reshape(ROWS // ROWS_DEV, ROWS_DEV)

    def one_block(block_pair):
        row_block, wanted = block_pair
        logits = lax.dot_general(row_block, weights, (((1,), (1,)), ((), ())), preferred_element_type=jnp.float32)
        highest = lax.optimization_barrier(jnp.max(logits, axis=1, keepdims=True))
        log_total = jnp.log(lax.optimization_barrier(jnp.sum(jnp.exp(logits - highest), axis=1))) + highest[:, 0]
        picked = jnp.take_along_axis(logits, wanted[:, None].astype(jnp.int32), axis=1)[:, 0]
        return picked - log_total
    return lax.map(one_block, (row_blocks, target_blocks)).reshape(ROWS)

def reference(gen_hidden, gen_gain, gen_head, dom_hidden, dom_gain, dom_head, targets, doc_ids):
    gen_logprob = log_probs(normalize(gen_hidden, gen_gain), gen_head, targets)
    dom_logprob = log_probs(normalize(dom_hidden, dom_gain), dom_head, targets)
    is_live = doc_ids >= 0
    token_diff = jnp.where(is_live, dom_logprob - gen_logprob, jnp.zeros_like(gen_logprob))
    onehot = (doc_ids[:, None] == jnp.arange(DOCS, dtype=jnp.int32)[None, :]).astype(jnp.float32)
    doc_sums = jnp.dot(token_diff, onehot, precision=lax.Precision.HIGHEST)
    counts = lax.optimization_barrier(jnp.sum(onehot, axis=0))
    return (token_diff, doc_sums / counts)
```

```python
import jax
import jax.numpy as jnp
from jax import lax
from jax.experimental import pallas as pl
from jax.experimental.pallas import tpu as pltpu
from jax.sharding import PartitionSpec as P

MESH = pl.DeviceIdType.MESH
F32 = jnp.float32
BF16 = jnp.bfloat16

PACKS = 8
PACK_ROWS = 128
DOC_PACK = 8
WIDTH = 4096
VOCAB_DEV = 1024
LANES = 128
BLOCKS = WIDTH // LANES
LIVE_ROWS = 544
THIRD_ROWS = (192, 176, 176)
THIRD_BASE = (0, 192, 368)
THIRD_PAD = 256
AXES = ((0, 1, 2), (1, 2, 0), (2, 0, 1))
LAG = 3


def turn(q):
    return q + q // 2 - 2 * (q // 3)


def device_of(x, y, z):
    return {"gen": (y // 2) * 4 + x, "dom": z * 2 + y % 2}


def slot_of(x, y, z):
    g, d = (y // 2) * 4 + x, z * 2 + y % 2
    odd = (x + y) % 2
    return (1 - odd) * (g * 4 + z) + odd * (BLOCKS + d * 4 + g // 2)


def remote(src, dst, send_sem, recv_sem, device):
    return pltpu.make_async_remote_copy(
        src_ref=src,
        dst_ref=dst,
        send_sem=send_sem,
        recv_sem=recv_sem,
        device_id=device,
        device_id_type=MESH,
    )


def kernel(
    gen_hidden,
    gen_gain,
    gen_head,
    dom_hidden,
    dom_gain,
    dom_head,
    targets,
    doc_ids,
    token_out,
    score_out,
    heads,
    x0,
    x1,
    x2,
    logits,
    place,
    normed,
    stage,
    hidden,
    gains,
    ids,
    square_in,
    square_full,
    square_src,
    square_src_full,
    stats_src,
    stats_in,
    total_src,
    total_in,
    want,
    load_sem,
    head_sem,
    stage_send,
    stage_recv,
    local_sem,
    square_send,
    square_recv,
    full_send,
    full_recv,
    full_local,
    ring_send,
    ring_recv,
    stats_send,
    stats_recv,
    total_send,
    total_recv,
):
    thirds = (x0, x1, x2)
    g, d = lax.axis_index("gen"), lax.axis_index("dom")
    core = lax.axis_index("dp")
    sign = 1 - 2 * core
    x, y, z = g % 4, (g // 4) * 2 + d % 2, d // 2
    here = (x, y, z)
    own_slot = slot_of(x, y, z)
    is_dom = (x + y) % 2
    own_block = own_slot % BLOCKS

    loads = [
        pltpu.make_async_copy(gen_hidden, hidden.at[0], load_sem.at[0]),
        pltpu.make_async_copy(dom_hidden, hidden.at[1], load_sem.at[1]),
        pltpu.make_async_copy(gen_gain, gains.at[0], load_sem.at[2]),
        pltpu.make_async_copy(dom_gain, gains.at[1], load_sem.at[3]),
        pltpu.make_async_copy(targets, ids.at[0], load_sem.at[4]),
        pltpu.make_async_copy(doc_ids, ids.at[1], load_sem.at[5]),
    ]
    for load in loads:
        load.start()

    barrier = pltpu.get_barrier_semaphore()
    for step in range(1, PACKS):
        pl.semaphore_signal(
            barrier, inc=1, device_id={"gen": (g + step) % PACKS}, device_id_type=MESH
        )
        pl.semaphore_signal(
            barrier, inc=1, device_id={"dom": (d + step) % PACKS}, device_id_type=MESH
        )
    pl.semaphore_signal(
        barrier,
        inc=1,
        device_id={"gen": (g + 4) % PACKS, "dom": d + 1 - 2 * (d % 2)},
        device_id_type=MESH,
    )
    pl.semaphore_wait(barrier, 2 * (PACKS - 1) + 1)

    gen_targets = [2 * q + g % 2 for q in range(4)]
    dom_targets = [2 * q + (d + 1) % 2 for q in range(4)]

    def stage_copy(q, model):
        cols = pl.ds(q * LANES, LANES)
        if model == 0:
            src, row, device = gen_hidden.at[:, cols], d, {"dom": gen_targets[q]}
        else:
            src, row, device = dom_hidden.at[:, cols], g, {"gen": dom_targets[q]}
        far = remote(
            src, stage.at[row], stage_send.at[model * 4 + q], stage_recv.at[row], device
        )
        near = pltpu.make_async_copy(src, stage.at[row], local_sem)
        return far, near

    def targets_self(q, model):
        return gen_targets[q] == d if model == 0 else dom_targets[q] == g

    def each_stage(act_far, act_near):
        for model in range(2):
            for q in range(4):
                mine = targets_self(q, model)
                far, near = stage_copy(q, model)
                if act_near is not None:
                    pl.when(mine)(lambda near=near: act_near(near))
                pl.when(jnp.logical_not(mine))(lambda far=far: act_far(far))

    each_stage(lambda c: c.start(), lambda c: c.start())

    loads[0].wait()
    loads[1].wait()
    for model in range(2):
        total = jnp.zeros((PACK_ROWS, LANES), F32)
        for q in range(4):
            part = hidden[model, :, q * LANES : (q + 1) * LANES].astype(F32)
            total = total + part * part
        row = jnp.sum(total.T, axis=0, keepdims=True)
        square_src[model] = row
        if model == 0:
            square_in[pl.ds(g, 1)] = row[None]
        else:
            square_in[pl.ds(PACKS + d, 1)] = row[None]

    def square_copy(step, model):
        if model == 0:
            device, own, other = {"gen": (g + step) % PACKS}, g, (g + PACKS - step) % PACKS
        else:
            device = {"dom": (d + step) % PACKS}
            own, other = PACKS + d, PACKS + (d + PACKS - step) % PACKS
        send = square_send.at[model * PACKS + step]
        out = remote(
            square_src.at[model], square_in.at[own], send, square_recv.at[own], device
        )
        arrival = remote(
            square_src.at[model], square_in.at[other], send, square_recv.at[other], device
        )
        return out, arrival

    for step in range(1, PACKS):
        for model in range(2):
            square_copy(step, model)[0].start()

    def load_heads(k, carry):
        cols = pl.ds(pl.multiple_of(k * LANES, LANES), LANES)
        pltpu.make_async_copy(gen_head.at[:, cols], heads.at[0, k], head_sem.at[0]).start()
        pltpu.make_async_copy(dom_head.at[:, cols], heads.at[1, k], head_sem.at[1]).start()
        return carry

    lax.fori_loop(0, BLOCKS, load_heads, 0)

    for step in range(1, PACKS):
        for model in range(2):
            square_copy(step, model)[1].wait_recv()
    for model in range(2):
        square_src_full[model] = jnp.sum(
            square_in[model * PACKS : (model + 1) * PACKS], axis=0
        )

    def full_copy(q, model):
        if model == 0:
            row, device = d, {"dom": gen_targets[q]}
        else:
            row, device = g, {"gen": dom_targets[q]}
        src = square_src_full.at[model]
        far = remote(src, square_full.at[row], full_send.at[model * 4 + q], full_recv.at[row], device)
        near = pltpu.make_async_copy(src, square_full.at[row], full_local)
        return far, near

    for model in range(2):
        for q in range(4):
            mine = targets_self(q, model)
            far, near = full_copy(q, model)
            pl.when(mine)(lambda near=near: near.start())
            pl.when(jnp.logical_not(mine))(lambda far=far: far.start())

    for load in loads[2:]:
        load.wait()
    docs = ids[1]
    counts = jnp.sum((docs >= 0).astype(jnp.int32), axis=1, keepdims=True)
    lane = lax.broadcasted_iota(jnp.int32, (THIRD_PAD, LANES), 1)
    sub = lax.broadcasted_iota(jnp.int32, (THIRD_PAD, LANES), 0)
    offset = jnp.zeros((1, 1), jnp.int32)
    for p in range(PACKS):
        count = counts[p : p + 1, :]
        for t in range(3):
            hit = jnp.logical_and(sub + (THIRD_BASE[t] - offset) == lane, lane < count)
            hit = jnp.logical_and(hit, sub < THIRD_ROWS[t])
            place[t, :, p * LANES : (p + 1) * LANES] = jnp.where(hit, 1.0, 0.0).astype(BF16)
        offset = offset + count

    first_column = (g * PACKS + d) * VOCAB_DEV
    tgt = ids[0]
    high, low = tgt // 256, tgt % 256
    pieces = []
    for t in range(3):
        got = jnp.zeros((32, THIRD_PAD), F32)
        for p in range(PACKS):
            rows = lax.broadcasted_iota(jnp.int32, (32, LANES), 0)
            pair = jnp.where(
                rows < 16,
                jnp.broadcast_to(high[p : p + 1, :], (32, LANES)),
                jnp.broadcast_to(low[p : p + 1, :], (32, LANES)),
            )
            got = got + lax.dot_general(
                pair.astype(F32).astype(BF16),
                place[t, :, p * LANES : (p + 1) * LANES],
                (((1,), (1,)), ((), ())),
                preferred_element_type=F32,
            )
        column = (got[0:8] * 256.0 + got[16:24]).astype(jnp.int32) - first_column
        want[t] = column

    def clear(slot, carry):
        for t in range(3):
            pad = THIRD_PAD - THIRD_ROWS[t]
            thirds[t][pl.ds(slot, 1), THIRD_ROWS[t] :, :] = jnp.zeros((1, pad, LANES), BF16)
        return carry

    lax.fori_loop(0, 2 * BLOCKS, clear, 0)

    def clear_logits(i, carry):
        rows = pl.ds(pl.multiple_of(i * 64, 64), 64)
        for a in range(6):
            logits[a, rows, :] = jnp.zeros((64, THIRD_PAD), F32)
        return carry

    lax.fori_loop(0, VOCAB_DEV // 64, clear_logits, 0)

    def source(p):
        return jnp.where(is_dom == 1, g, d) == p

    for p in range(PACKS):
        mine = source(p)

        @pl.when(jnp.logical_not(mine))
        def _(p=p):
            remote(
                stage.at[p], stage.at[p], stage_send.at[0], stage_recv.at[p], {"dom": d}
            ).wait_recv()
            remote(
                square_full.at[p], square_full.at[p], full_send.at[0], full_recv.at[p], {"dom": d}
            ).wait_recv()

        @pl.when(mine)
        def _(p=p):
            pltpu.make_async_copy(stage.at[p], stage.at[p], local_sem).wait()
            pltpu.make_async_copy(square_full.at[p], square_full.at[p], full_local).wait()

    gain = gains[is_dom, pl.ds(own_block, 1), :]
    for p in range(PACKS):
        scale = lax.rsqrt(square_full[p] / WIDTH + 1e-05)
        scale = jnp.broadcast_to(scale, (PACK_ROWS, LANES)).T
        values = stage[p].astype(F32) * scale * gain
        normed[p * PACK_ROWS : (p + 1) * PACK_ROWS, :] = values.astype(BF16)
    for t in range(3):
        rows = jnp.dot(place[t], normed[...], preferred_element_type=F32).astype(BF16)
        thirds[t][pl.ds(own_slot, 1)] = rows[None]

    def moved(axis, by):
        at = list(here)
        at[axis] = (at[axis] + by + 4) % 4
        return device_of(*at)

    ahead = [moved(axis, sign) for axis in range(3)]
    behind = [moved(axis, -sign) for axis in range(3)]

    def slot_at(t, u):
        at = list(here)
        for k in range(3):
            axis = AXES[t][k]
            at[axis] = (at[axis] - sign * u[k] + 4) % 4
        return slot_of(*at)

    def piece(t, u):
        return thirds[t].at[slot_at(t, u), pl.ds(0, THIRD_ROWS[t])]

    def ring_index(t, u):
        return t * 64 + u[0] * 16 + u[1] * 4 + u[2]

    def push(t, u, k, forward):
        new = list(u)
        new[k] = new[k] + 1 if forward else 3
        device = (ahead if forward else behind)[AXES[t][k]]
        ref = piece(t, u)
        remote(ref, ref, ring_send.at[t], ring_recv.at[ring_index(t, new)], device).start()

    def arrived(t, u):
        ref = piece(t, u)
        remote(ref, ref, ring_send.at[t], ring_recv.at[ring_index(t, u)], ahead[0]).wait_recv()

    for k in range(3):
        for t in range(3):
            push(t, (0, 0, 0), k, True)
            push(t, (0, 0, 0), k, False)
    for first in (1, 3, 2):
        for t in range(3):
            u = (first, 0, 0)
            arrived(t, u)
            if first == 1:
                push(t, u, 0, True)
            for k in (1, 2):
                push(t, u, k, True)
                push(t, u, k, False)
    for second in (1, 3, 2):

        def middle(i, carry, second=second):
            for t in range(3):
                u = (turn(i), second, 0)
                arrived(t, u)
                if second == 1:
                    push(t, u, 1, True)
                push(t, u, 2, True)
                push(t, u, 2, False)
            return carry

        lax.fori_loop(0, 4, middle, 0)

    def relay(n):
        for t in range(3):
            u = (turn(n % 4), turn(n // 4), 1)
            arrived(t, u)
            push(t, u, 2, True)

    def gather_slots(t, n):
        return [slot_at(t, (turn(n % 4), turn(n // 4), u)) for u in range(4)]

    def multiply(t, slots):
        model = slots[0] // BLOCKS
        left = jnp.concatenate([heads[model, s % BLOCKS] for s in slots], axis=1)
        right = jnp.concatenate([thirds[t][s] for s in slots], axis=1)
        return model, lax.dot_general(
            left, right, (((1,), (1,)), ((), ())), preferred_element_type=F32
        )

    def add_line(n):
        for t in range(3):
            for last in (3, 2):
                arrived(t, (turn(n % 4), turn(n // 4), last))
            s = gather_slots(t, n)
            groups = [s] if AXES[t][2] == 2 else [[s[0], s[2]], [s[1], s[3]]]
            for group in groups:
                model, product = multiply(t, group)
                logits[2 * t + model] += product

    pltpu.make_async_copy(heads.at[0], heads.at[0], head_sem.at[0]).wait()
    pltpu.make_async_copy(heads.at[1], heads.at[1], head_sem.at[1]).wait()

    def lead(n, carry):
        relay(n)
        return carry

    def steady(n, carry):
        relay(n + LAG)
        add_line(n)
        return carry

    def drain(n, carry):
        add_line(n)
        return carry

    lax.fori_loop(0, LAG, lead, 0)
    lax.fori_loop(0, 16 - LAG, steady, 0)
    lax.fori_loop(16 - LAG, 16, drain, 0)

    CHUNK = 64
    steps = VOCAB_DEV // CHUNK
    spread = jnp.zeros((32, VOCAB_DEV), F32)
    for t in range(3):

        def highest(i, so_far, t=t):
            rows = pl.ds(pl.multiple_of(i * CHUNK, CHUNK), CHUNK)
            out = []
            for model in range(2):
                block = logits[2 * t + model, rows, :].reshape(CHUNK // 8, 8, THIRD_PAD)
                out.append(jnp.maximum(so_far[model], jnp.max(block, axis=0)))
            return tuple(out)

        least = jnp.full((8, THIRD_PAD), -jnp.inf, F32)
        tops = lax.fori_loop(0, steps, highest, (least, least))
        tops = [jnp.max(top, axis=0, keepdims=True) for top in tops]
        wanted = want[t]

        def totals(i, so_far, t=t, tops=tops, wanted=wanted):
            rows = pl.ds(pl.multiple_of(i * CHUNK, CHUNK), CHUNK)
            gen = logits[2 * t, rows, :].reshape(CHUNK // 8, 8, THIRD_PAD)
            dom = logits[2 * t + 1, rows, :].reshape(CHUNK // 8, 8, THIRD_PAD)
            gen_sum = so_far[0] + jnp.sum(jnp.exp(gen - tops[0][None]), axis=0)
            dom_sum = so_far[1] + jnp.sum(jnp.exp(dom - tops[1][None]), axis=0)
            entry = (
                lax.broadcasted_iota(jnp.int32, (CHUNK // 8, 8, THIRD_PAD), 0) * 8
                + lax.broadcasted_iota(jnp.int32, (CHUNK // 8, 8, THIRD_PAD), 1)
                + i * CHUNK
            )
            picked = so_far[2] + jnp.sum(
                jnp.where(entry == wanted[None], dom - gen, 0.0), axis=0
            )
            return gen_sum, dom_sum, picked

        zero = jnp.zeros((8, THIRD_PAD), F32)
        sums = lax.fori_loop(0, steps, totals, (zero, zero, zero))
        sums = [jnp.sum(value, axis=0, keepdims=True) for value in sums]
        values = [tops[0] + jnp.log(sums[0]), tops[1] + jnp.log(sums[1]), sums[2]]
        row = lax.broadcasted_iota(jnp.int32, (32, THIRD_PAD), 0)
        stack = jnp.zeros((32, THIRD_PAD), F32)
        for k in range(3):
            rest = values[k]
            for part in range(3):
                head = rest.astype(BF16).astype(F32)
                stack = jnp.where(row == part * 8 + k, head, stack)
                rest = rest - head
        spread = spread + jnp.dot(stack.astype(BF16), place[t], preferred_element_type=F32)
    spread = spread[0:8] + spread[8:16] + spread[16:24]
    for p in range(PACKS):
        stats_src[p] = spread[:, p * LANES : (p + 1) * LANES]

    def combine(block):
        top = jnp.max(block, axis=0)
        total = top + jnp.log(jnp.sum(jnp.exp(block - top[None]), axis=0))
        row = lax.broadcasted_iota(jnp.int32, (8, LANES), 0)
        return jnp.where(row < 2, total, jnp.sum(block, axis=0))

    def stats_copy(step):
        to, other = (d + step) % PACKS, (d + PACKS - step) % PACKS
        out = remote(
            stats_src.at[to], stats_in.at[d], stats_send.at[step], stats_recv.at[d], {"dom": to}
        )
        arrival = remote(
            stats_src.at[to], stats_in.at[other], stats_send.at[step], stats_recv.at[other], {"dom": to}
        )
        return out, arrival

    for step in range(1, PACKS):
        stats_copy(step)[0].start()
    stats_in[pl.ds(d, 1)] = stats_src[pl.ds(d, 1)]
    for step in range(1, PACKS):
        stats_copy(step)[1].wait_recv()
    partial = combine(stats_in[...])
    total_src[...] = partial
    total_in[pl.ds(g, 1)] = partial[None]

    def total_copy(step):
        to, other = (g + step) % PACKS, (g + PACKS - step) % PACKS
        out = remote(
            total_src, total_in.at[g], total_send.at[step], total_recv.at[g], {"gen": to}
        )
        arrival = remote(
            total_src, total_in.at[other], total_send.at[step], total_recv.at[other], {"gen": to}
        )
        return out, arrival

    for step in range(1, PACKS):
        total_copy(step)[0].start()

    each_stage(lambda c: c.wait_send(), None)
    for model in range(2):
        for q in range(4):
            mine = targets_self(q, model)
            far, _ = full_copy(q, model)
            pl.when(jnp.logical_not(mine))(lambda far=far: far.wait_send())
    for step in range(1, PACKS):
        for model in range(2):
            square_copy(step, model)[0].wait_send()
        stats_copy(step)[0].wait_send()
    for t in range(3):
        ref = thirds[t].at[pl.ds(0, 63), pl.ds(0, THIRD_ROWS[t])]
        remote(ref, ref, ring_send.at[t], ring_recv.at[0], ahead[0]).wait_send()

    for step in range(1, PACKS):
        total_copy(step)[1].wait_recv()
    final = combine(total_in[...])
    token = final[2:3] - final[1:2] + final[0:1]
    own_docs = ids[1, pl.ds(d, 1), :]
    token = jnp.where(own_docs >= 0, token, 0.0)
    token_out[...] = token
    row = lax.broadcasted_iota(jnp.int32, (DOC_PACK, LANES), 0)
    col = lax.broadcasted_iota(jnp.int32, (DOC_PACK, LANES), 1)
    member = (own_docs - d * DOC_PACK) == row
    doc_sum = jnp.sum(jnp.where(member, token, 0.0), axis=1, keepdims=True)
    doc_count = jnp.sum(jnp.where(member, 1.0, 0.0), axis=1, keepdims=True)
    score = jnp.sum(jnp.where(row == col, doc_sum / doc_count, 0.0), axis=0, keepdims=True)
    score_out[...] = score[:, :DOC_PACK]

    for step in range(1, PACKS):
        total_copy(step)[0].wait_send()


def per_device(gen_hidden, gen_gain, gen_head, dom_hidden, dom_gain, dom_head, targets, doc_ids):
    anywhere = pl.BlockSpec(memory_space=pl.ANY)
    dma = pltpu.SemaphoreType.DMA
    slots = pltpu.VMEM((2 * BLOCKS, THIRD_PAD, LANES), BF16)
    token, score = pl.pallas_call(
        kernel,
        out_shape=(
            jax.ShapeDtypeStruct((1, PACK_ROWS), F32),
            jax.ShapeDtypeStruct((1, DOC_PACK), F32),
        ),
        in_specs=[anywhere] * 8,
        out_specs=(
            pl.BlockSpec(memory_space=pltpu.VMEM),
            pl.BlockSpec(memory_space=pltpu.VMEM),
        ),
        scratch_shapes=[
            pltpu.VMEM((2, BLOCKS, VOCAB_DEV, LANES), BF16),
            slots,
            slots,
            slots,
            pltpu.VMEM((6, VOCAB_DEV, THIRD_PAD), F32),
            pltpu.VMEM((3, THIRD_PAD, PACKS * PACK_ROWS), BF16),
            pltpu.VMEM((PACKS * PACK_ROWS, LANES), BF16),
            pltpu.VMEM((PACKS, PACK_ROWS, LANES), BF16),
            pltpu.VMEM((2, PACK_ROWS, 4 * LANES), BF16),
            pltpu.VMEM((2, BLOCKS, LANES), F32),
            pltpu.VMEM((2, PACKS, LANES), jnp.int32),
            pltpu.VMEM((2 * PACKS, 1, LANES), F32),
            pltpu.VMEM((PACKS, 1, LANES), F32),
            pltpu.VMEM((2, 1, LANES), F32),
            pltpu.VMEM((2, 1, LANES), F32),
            pltpu.VMEM((PACKS, 8, LANES), F32),
            pltpu.VMEM((PACKS, 8, LANES), F32),
            pltpu.VMEM((8, LANES), F32),
            pltpu.VMEM((PACKS, 8, LANES), F32),
            pltpu.VMEM((3, 8, THIRD_PAD), jnp.int32),
            dma((6,)),
            dma((2,)),
            dma((8,)),
            dma((8,)),
            dma,
            dma((16,)),
            dma((16,)),
            dma((8,)),
            dma((8,)),
            dma,
            dma((3,)),
            dma((192,)),
            dma((8,)),
            dma((8,)),
            dma((8,)),
            dma((8,)),
        ],
        compiler_params=pltpu.CompilerParams(
            collective_id=0, has_side_effects=True, vmem_limit_bytes=60 * 1024 * 1024
        ),
        cost_estimate=pl.CostEstimate(
            flops=4 * LIVE_ROWS * VOCAB_DEV * WIDTH,
            bytes_accessed=4 * VOCAB_DEV * WIDTH,
            transcendentals=2 * LIVE_ROWS * VOCAB_DEV,
        ),
    )(
        gen_hidden,
        gen_gain.reshape(BLOCKS, LANES),
        gen_head,
        dom_hidden,
        dom_gain.reshape(BLOCKS, LANES),
        dom_head,
        targets.reshape(PACKS, LANES),
        doc_ids.reshape(PACKS, LANES),
    )
    return token.reshape(PACK_ROWS), score.reshape(DOC_PACK)


def solution(mesh):
    in_specs = (
        P(("dp", "dom"), "gen"),
        P("dp"),
        P(("dp", "gen", "dom"), None),
        P(("dp", "gen"), "dom"),
        P("dp"),
        P(("dp", "gen", "dom"), None),
        P("dp"),
        P("dp"),
    )
    out_specs = (P(("dp", "dom")), P(("dp", "dom")))
    return jax.shard_map(
        per_device, mesh=mesh, in_specs=in_specs, out_specs=out_specs, check_vma=False
    )
```

```python
import jax
import jax.numpy as jnp
from jax import lax
from jax.experimental import pallas as pl
from jax.experimental.pallas import tpu as pltpu
from jax.sharding import PartitionSpec as P

MESH = pl.DeviceIdType.MESH
F32 = jnp.float32
BF16 = jnp.bfloat16

PACKS = 8
PACK_ROWS = 128
DOC_PACK = 8
WIDTH = 4096
VOCAB_DEV = 1024
LANES = 128
BLOCKS = WIDTH // LANES
LIVE_ROWS = 544
THIRD_ROWS = (192, 176, 176)
THIRD_BASE = (0, 192, 368)
THIRD_PAD = 256
AXES = ((0, 1, 2), (1, 2, 0), (2, 0, 1))


def turn(q):
    return q + q // 2 - 2 * (q // 3)


def device_of(x, y, z):
    return {"gen": (y // 2) * 4 + x, "dom": z * 2 + y % 2}


def slot_of(x, y, z):
    g, d = (y // 2) * 4 + x, z * 2 + y % 2
    odd = (x + y) % 2
    return (1 - odd) * (g * 4 + z) + odd * (BLOCKS + d * 4 + g // 2)


def remote(src, dst, send_sem, recv_sem, device):
    return pltpu.make_async_remote_copy(
        src_ref=src,
        dst_ref=dst,
        send_sem=send_sem,
        recv_sem=recv_sem,
        device_id=device,
        device_id_type=MESH,
    )


def kernel(
    gen_hidden,
    gen_gain,
    gen_head,
    dom_hidden,
    dom_gain,
    dom_head,
    targets,
    doc_ids,
    total_out,
    heads,
    x0,
    x1,
    x2,
    logits,
    place,
    stage,
    hidden,
    gains,
    ids,
    square_in,
    square_full,
    square_src,
    square_src_full,
    scale_parts,
    scales,
    stats_src,
    stats_in,
    want,
    load_sem,
    head_sem,
    stage_send,
    stage_recv,
    local_sem,
    square_send,
    square_recv,
    full_send,
    full_recv,
    ring_send,
    ring_recv,
    stats_send,
    stats_recv,
):
    thirds = (x0, x1, x2)
    g, d = lax.axis_index("gen"), lax.axis_index("dom")
    core = lax.axis_index("dp")
    sign = 1 - 2 * core
    x, y, z = g % 4, (g // 4) * 2 + d % 2, d // 2
    here = (x, y, z)
    own_slot = slot_of(x, y, z)
    is_dom = (x + y) % 2

    barrier = pltpu.get_barrier_semaphore()
    for step in range(1, PACKS):
        pl.semaphore_signal(
            barrier, inc=1, device_id={"gen": (g + step) % PACKS}, device_id_type=MESH
        )
        pl.semaphore_signal(
            barrier, inc=1, device_id={"dom": (d + step) % PACKS}, device_id_type=MESH
        )
    pl.semaphore_signal(
        barrier,
        inc=1,
        device_id={"gen": (g + 4) % PACKS, "dom": d + 1 - 2 * (d % 2)},
        device_id_type=MESH,
    )

    loads = [
        pltpu.make_async_copy(gen_hidden, hidden.at[0], load_sem.at[0]),
        pltpu.make_async_copy(dom_hidden, hidden.at[1], load_sem.at[1]),
        pltpu.make_async_copy(gen_gain, gains.at[0], load_sem.at[2]),
        pltpu.make_async_copy(dom_gain, gains.at[1], load_sem.at[3]),
        pltpu.make_async_copy(targets, ids.at[0], load_sem.at[4]),
        pltpu.make_async_copy(doc_ids, ids.at[1], load_sem.at[5]),
    ]
    for load in loads:
        load.start()

    loads[0].wait()
    loads[1].wait()
    for model in range(2):
        total = jnp.zeros((PACK_ROWS, LANES), F32)
        for q in range(4):
            part = hidden[model, :, q * LANES : (q + 1) * LANES].astype(F32)
            total = total + part * part
        row = jnp.sum(total.T, axis=0, keepdims=True)
        square_src[model] = row
        if model == 0:
            square_in[pl.ds(g, 1)] = row[None]
        else:
            square_in[pl.ds(PACKS + d, 1)] = row[None]

    pl.semaphore_wait(barrier, 2 * (PACKS - 1) + 1)

    gen_targets = [2 * q + g % 2 for q in range(4)]
    dom_targets = [2 * q + (d + 1) % 2 for q in range(4)]

    def stage_copy(q, model):
        cols = pl.ds(q * LANES, LANES)
        if model == 0:
            src, row, device = gen_hidden.at[:, cols], d, {"dom": gen_targets[q]}
        else:
            src, row, device = dom_hidden.at[:, cols], g, {"gen": dom_targets[q]}
        far = remote(
            src, stage.at[row], stage_send.at[model * 4 + q], stage_recv.at[row], device
        )
        near = pltpu.make_async_copy(src, stage.at[row], local_sem)
        return far, near

    def targets_self(q, model):
        return gen_targets[q] == d if model == 0 else dom_targets[q] == g

    def each_stage(act_far, act_near):
        for model in range(2):
            for q in range(4):
                mine = targets_self(q, model)
                far, near = stage_copy(q, model)
                if act_near is not None:
                    pl.when(mine)(lambda near=near: act_near(near))
                pl.when(jnp.logical_not(mine))(lambda far=far: act_far(far))

    each_stage(lambda c: c.start(), lambda c: c.start())

    def square_copy(step, model):
        if model == 0:
            device, own, other = {"gen": (g + step) % PACKS}, g, (g + PACKS - step) % PACKS
        else:
            device = {"dom": (d + step) % PACKS}
            own, other = PACKS + d, PACKS + (d + PACKS - step) % PACKS
        send = square_send.at[model * PACKS + step]
        out = remote(
            square_src.at[model], square_in.at[own], send, square_recv.at[own], device
        )
        arrival = remote(
            square_src.at[model], square_in.at[other], send, square_recv.at[other], device
        )
        return out, arrival

    for step in range(1, PACKS):
        for model in range(2):
            square_copy(step, model)[0].start()

    def load_heads(k, carry):
        cols = pl.ds(pl.multiple_of(k * LANES, LANES), LANES)
        pltpu.make_async_copy(gen_head.at[:, cols], heads.at[0, k], head_sem.at[0]).start()
        pltpu.make_async_copy(dom_head.at[:, cols], heads.at[1, k], head_sem.at[1]).start()
        return carry

    lax.fori_loop(0, BLOCKS, load_heads, 0)

    for step in range(1, PACKS):
        for model in range(2):
            square_copy(step, model)[1].wait_recv()
    for model in range(2):
        row = jnp.sum(square_in[model * PACKS : (model + 1) * PACKS], axis=0)
        square_src_full[model] = row
        own = d if model == 0 else PACKS + g
        square_full[pl.ds(own, 1)] = row[None]

    def full_copy(step, model):
        back = PACKS - step
        if model == 0:
            device, own, other = {"dom": (d + step) % PACKS}, d, (d + back) % PACKS
        else:
            device = {"gen": (g + step) % PACKS}
            own, other = PACKS + g, PACKS + (g + back) % PACKS
        src, send = square_src_full.at[model], full_send.at[model * PACKS + step]
        out = remote(src, square_full.at[own], send, full_recv.at[own], device)
        arrival = remote(src, square_full.at[other], send, full_recv.at[other], device)
        return out, arrival

    for step in range(1, PACKS):
        for model in range(2):
            full_copy(step, model)[0].start()

    for load in loads[2:]:
        load.wait()
    docs = ids[1]
    counts = jnp.sum((docs >= 0).astype(jnp.int32), axis=1, keepdims=True)
    lane = lax.broadcasted_iota(jnp.int32, (THIRD_PAD, LANES), 1)
    sub = lax.broadcasted_iota(jnp.int32, (THIRD_PAD, LANES), 0)
    offset = jnp.zeros((1, 1), jnp.int32)
    for p in range(PACKS):
        count = counts[p : p + 1, :]
        for t in range(3):
            hit = jnp.logical_and(sub + (THIRD_BASE[t] - offset) == lane, lane < count)
            hit = jnp.logical_and(hit, sub < THIRD_ROWS[t])
            place[t, :, p * LANES : (p + 1) * LANES] = jnp.where(hit, 1.0, 0.0).astype(BF16)
        offset = offset + count

    first_column = (g * PACKS + d) * VOCAB_DEV
    tgt = ids[0]
    high, low = tgt // 256, tgt % 256
    pieces = []
    for t in range(3):
        got = jnp.zeros((32, THIRD_PAD), F32)
        for p in range(PACKS):
            rows = lax.broadcasted_iota(jnp.int32, (32, LANES), 0)
            pair = jnp.where(
                rows < 16,
                jnp.broadcast_to(high[p : p + 1, :], (32, LANES)),
                jnp.broadcast_to(low[p : p + 1, :], (32, LANES)),
            )
            got = got + lax.dot_general(
                pair.astype(F32).astype(BF16),
                place[t, :, p * LANES : (p + 1) * LANES],
                (((1,), (1,)), ((), ())),
                preferred_element_type=F32,
            )
        column = (got[0:8] * 256.0 + got[16:24]).astype(jnp.int32) - first_column
        want[t] = column

    def clear(slot, carry):
        for t in range(3):
            pad = THIRD_PAD - THIRD_ROWS[t]
            thirds[t][pl.ds(slot, 1), THIRD_ROWS[t] :, :] = jnp.zeros((1, pad, LANES), BF16)
        return carry

    lax.fori_loop(0, 2 * BLOCKS, clear, 0)

    def clear_logits(i, carry):
        rows = pl.ds(pl.multiple_of(i * 64, 64), 64)
        for a in range(6):
            logits[a, rows, :] = jnp.zeros((64, THIRD_PAD), F32)
        return carry

    lax.fori_loop(0, VOCAB_DEV // 64, clear_logits, 0)

    def source(p):
        return jnp.where(is_dom == 1, g, d) == p

    for p in range(PACKS):
        mine = source(p)

        @pl.when(jnp.logical_not(mine))
        def _(p=p):
            remote(
                stage.at[p], stage.at[p], stage_send.at[0], stage_recv.at[p], {"dom": d}
            ).wait_recv()

        @pl.when(mine)
        def _(p=p):
            pltpu.make_async_copy(stage.at[p], stage.at[p], local_sem).wait()

    for t in range(3):
        rows = jnp.dot(
            place[t],
            stage[...].reshape(PACKS * PACK_ROWS, LANES),
            preferred_element_type=F32,
        ).astype(BF16)
        thirds[t][pl.ds(own_slot, 1)] = rows[None]

    def moved(axis, by):
        at = list(here)
        at[axis] = (at[axis] + by + 4) % 4
        return device_of(*at)

    ahead = [moved(axis, sign) for axis in range(3)]
    behind = [moved(axis, -sign) for axis in range(3)]

    def slot_at(t, u):
        at = list(here)
        for k in range(3):
            axis = AXES[t][k]
            at[axis] = (at[axis] - sign * u[k] + 4) % 4
        return slot_of(*at)

    def piece(t, u):
        return thirds[t].at[slot_at(t, u), pl.ds(0, THIRD_ROWS[t])]

    def ring_index(t, u):
        return t * 64 + u[0] * 16 + u[1] * 4 + u[2]

    def push(t, u, k, forward):
        new = list(u)
        new[k] = new[k] + 1 if forward else 3
        device = (ahead if forward else behind)[AXES[t][k]]
        ref = piece(t, u)
        remote(ref, ref, ring_send.at[t], ring_recv.at[ring_index(t, new)], device).start()

    def arrived(t, u):
        ref = piece(t, u)
        remote(ref, ref, ring_send.at[t], ring_recv.at[ring_index(t, u)], ahead[0]).wait_recv()

    for k in range(3):
        for t in range(3):
            push(t, (0, 0, 0), k, True)
            push(t, (0, 0, 0), k, False)

    for step in range(1, PACKS):
        for model in range(2):
            full_copy(step, model)[1].wait_recv()
    for model in range(2):
        for p in range(PACKS):
            rest = lax.rsqrt(square_full[model * PACKS + p] / WIDTH + 1e-05)
            rest = jnp.broadcast_to(rest, (PACK_ROWS, LANES)).T
            for part in range(3):
                head = rest.astype(BF16)
                scale_parts[part, p * PACK_ROWS : (p + 1) * PACK_ROWS, :] = head
                rest = rest - head.astype(F32)
        for t in range(3):
            total = jnp.zeros((THIRD_PAD, LANES), F32)
            for part in range(3):
                total = total + jnp.dot(
                    place[t], scale_parts[part], preferred_element_type=F32
                )
            scales[2 * t + model] = total

    for first in (1, 3, 2):
        for t in range(3):
            u = (first, 0, 0)
            arrived(t, u)
            if first == 1:
                push(t, u, 0, True)
            push(t, u, 1, True)
            push(t, u, 1, False)
    for first in (1, 3, 2):
        for t in range(3):
            push(t, (first, 0, 0), 2, True)
            push(t, (first, 0, 0), 2, False)

    def line(n, last):
        return turn(n % 4), turn(n // 4), last

    def announce(t, n):
        push(t, line(n, 0), 2, True)
        push(t, line(n, 0), 2, False)

    def relay(t, n):
        arrived(t, line(n, 1))
        push(t, line(n, 1), 2, True)

    def middle(i, carry):
        for t in range(3):
            u = (turn(i), 1, 0)
            arrived(t, u)
            push(t, u, 1, True)
            push(t, u, 2, True)
            push(t, u, 2, False)
        return carry

    lax.fori_loop(0, 4, middle, 0)

    def add_layer(t, half, last):
        slots = [slot_at(t, line(8 * half + i, last)) for i in range(8)]
        if t == 0:
            order = (0, 3, 5, 6, 1, 2, 4, 7)
        elif t == 1:
            order = (0, 3, 4, 7, 1, 2, 5, 6)
        else:
            order = (0, 1, 2, 3, 4, 5, 6, 7)
        for group in (order[:4], order[4:]):
            group = [slots[i] for i in group]
            model = group[0] // BLOCKS
            left = jnp.concatenate([heads[model, s % BLOCKS] for s in group], axis=1)
            scale = scales[2 * t + model]
            right = jnp.concatenate(
                [
                    (
                        thirds[t][s].astype(F32) * scale * gains[model, pl.ds(s % BLOCKS, 1), :]
                    ).astype(BF16)
                    for s in group
                ],
                axis=1,
            )
            logits[2 * t + model] += lax.dot_general(
                left, right, (((1,), (1,)), ((), ())), preferred_element_type=F32
            )

    pltpu.make_async_copy(heads.at[0], heads.at[0], head_sem.at[0]).wait()
    pltpu.make_async_copy(heads.at[1], heads.at[1], head_sem.at[1]).wait()

    def layer(k, carry):
        half = jnp.where((k == 3) | (k >= 5), 1, 0)
        last = jnp.where((k == 1) | (k == 5), 3, 0)
        last = jnp.where((k == 2) | (k == 6), 1, last)
        last = jnp.where((k == 4) | (k == 7), 2, last)
        for t in range(3):

            @pl.when(last >= 2)
            def _(t=t):
                for i in range(8):
                    arrived(t, line(8 * half + i, last))

            add_layer(t, half, last)

            @pl.when(k < 2)
            def _(t=t):
                for i in range(4):
                    n = 8 + 4 * k + i
                    arrived(t, line(n, 0))
                    announce(t, n)

            @pl.when((k < 2) | (k == 3) | (k == 4))
            def _(t=t):
                for i in range(4):
                    relay(t, 4 * (k - k // 3) + i)

        return carry

    lax.fori_loop(0, 8, layer, 0)

    CHUNK = 64
    steps = VOCAB_DEV // CHUNK
    spread = jnp.zeros((32, VOCAB_DEV), F32)
    for t in range(3):

        def highest(i, so_far, t=t):
            rows = pl.ds(pl.multiple_of(i * CHUNK, CHUNK), CHUNK)
            out = []
            for model in range(2):
                block = logits[2 * t + model, rows, :].reshape(CHUNK // 8, 8, THIRD_PAD)
                out.append(jnp.maximum(so_far[model], jnp.max(block, axis=0)))
            return tuple(out)

        least = jnp.full((8, THIRD_PAD), -jnp.inf, F32)
        tops = lax.fori_loop(0, steps, highest, (least, least))
        tops = [jnp.max(top, axis=0, keepdims=True) for top in tops]
        wanted = want[t]

        def totals(i, so_far, t=t, tops=tops, wanted=wanted):
            rows = pl.ds(pl.multiple_of(i * CHUNK, CHUNK), CHUNK)
            gen = logits[2 * t, rows, :].reshape(CHUNK // 8, 8, THIRD_PAD)
            dom = logits[2 * t + 1, rows, :].reshape(CHUNK // 8, 8, THIRD_PAD)
            gen_sum = so_far[0] + jnp.sum(jnp.exp(gen - tops[0][None]), axis=0)
            dom_sum = so_far[1] + jnp.sum(jnp.exp(dom - tops[1][None]), axis=0)
            entry = (
                lax.broadcasted_iota(jnp.int32, (CHUNK // 8, 8, THIRD_PAD), 0) * 8
                + lax.broadcasted_iota(jnp.int32, (CHUNK // 8, 8, THIRD_PAD), 1)
                + i * CHUNK
            )
            picked = so_far[2] + jnp.sum(
                jnp.where(entry == wanted[None], dom - gen, 0.0), axis=0
            )
            return gen_sum, dom_sum, picked

        zero = jnp.zeros((8, THIRD_PAD), F32)
        sums = lax.fori_loop(0, steps, totals, (zero, zero, zero))
        sums = [jnp.sum(value, axis=0, keepdims=True) for value in sums]
        values = [tops[0] + jnp.log(sums[0]), tops[1] + jnp.log(sums[1]), sums[2]]
        row = lax.broadcasted_iota(jnp.int32, (32, THIRD_PAD), 0)
        stack = jnp.zeros((32, THIRD_PAD), F32)
        for k in range(3):
            rest = values[k]
            for part in range(3):
                head = rest.astype(BF16).astype(F32)
                stack = jnp.where(row == part * 8 + k, head, stack)
                rest = rest - head
        spread = spread + jnp.dot(stack.astype(BF16), place[t], preferred_element_type=F32)
    spread = spread[0:8] + spread[8:16] + spread[16:24]
    for p in range(PACKS):
        stats_src[p] = spread[0:4, p * LANES : (p + 1) * LANES]

    me = g * PACKS + d

    def share(step, carry):
        peer = (me + step) % (PACKS * PACKS)
        remote(
            stats_src.at[peer % PACKS],
            stats_in.at[me],
            stats_send,
            stats_recv,
            {"gen": peer // PACKS, "dom": peer % PACKS},
        ).start()
        return carry

    lax.fori_loop(1, PACKS * PACKS, share, 0)
    stats_in[pl.ds(me, 1)] = stats_src[pl.ds(d, 1)]

    each_stage(lambda c: c.wait_send(), None)
    for step in range(1, PACKS):
        for model in range(2):
            square_copy(step, model)[0].wait_send()
            full_copy(step, model)[0].wait_send()
    for t in range(3):
        ref = thirds[t].at[pl.ds(0, 63), pl.ds(0, THIRD_ROWS[t])]
        remote(ref, ref, ring_send.at[t], ring_recv.at[0], ahead[0]).wait_send()

    others = stats_in.at[pl.ds(0, PACKS * PACKS - 1)]
    remote(others, others, stats_send, stats_recv, ahead[0]).wait()
    block = stats_in[...]
    top = jnp.max(block, axis=0)
    total = top + jnp.log(jnp.sum(jnp.exp(block - top[None]), axis=0))
    row = lax.broadcasted_iota(jnp.int32, (4, LANES), 0)
    total_out[...] = jnp.where(row < 2, total, jnp.sum(block, axis=0))


def finish(total, doc_ids, token_out, score_out):
    d = lax.axis_index("dom")
    token = total[2:3, :] - total[1:2, :] + total[0:1, :]
    own_docs = doc_ids[pl.ds(d, 1), :]
    token = jnp.where(own_docs >= 0, token, 0.0)
    token_out[...] = token
    row = lax.broadcasted_iota(jnp.int32, (DOC_PACK, LANES), 0)
    col = lax.broadcasted_iota(jnp.int32, (DOC_PACK, LANES), 1)
    member = (own_docs - d * DOC_PACK) == row
    doc_sum = jnp.sum(jnp.where(member, token, 0.0), axis=1, keepdims=True)
    doc_count = jnp.sum(jnp.where(member, 1.0, 0.0), axis=1, keepdims=True)
    score = jnp.sum(jnp.where(row == col, doc_sum / doc_count, 0.0), axis=0, keepdims=True)
    score_out[...] = score[:, :DOC_PACK]


def per_device(gen_hidden, gen_gain, gen_head, dom_hidden, dom_gain, dom_head, targets, doc_ids):
    anywhere = pl.BlockSpec(memory_space=pl.ANY)
    dma = pltpu.SemaphoreType.DMA
    slots = pltpu.VMEM((2 * BLOCKS, THIRD_PAD, LANES), BF16)
    docs = doc_ids.reshape(PACKS, LANES)
    total = pl.pallas_call(
        kernel,
        out_shape=jax.ShapeDtypeStruct((4, LANES), F32),
        in_specs=[anywhere] * 8,
        out_specs=pl.BlockSpec(memory_space=pltpu.VMEM),
        scratch_shapes=[
            pltpu.VMEM((2, BLOCKS, VOCAB_DEV, LANES), BF16),
            slots,
            slots,
            slots,
            pltpu.VMEM((6, VOCAB_DEV, THIRD_PAD), F32),
            pltpu.VMEM((3, THIRD_PAD, PACKS * PACK_ROWS), BF16),
            pltpu.VMEM((PACKS, PACK_ROWS, LANES), BF16),
            pltpu.VMEM((2, PACK_ROWS, 4 * LANES), BF16),
            pltpu.VMEM((2, BLOCKS, LANES), F32),
            pltpu.VMEM((2, PACKS, LANES), jnp.int32),
            pltpu.VMEM((2 * PACKS, 1, LANES), F32),
            pltpu.VMEM((2 * PACKS, 1, LANES), F32),
            pltpu.VMEM((2, 1, LANES), F32),
            pltpu.VMEM((2, 1, LANES), F32),
            pltpu.VMEM((3, PACKS * PACK_ROWS, LANES), BF16),
            pltpu.VMEM((6, THIRD_PAD, LANES), F32),
            pltpu.VMEM((PACKS, 4, LANES), F32),
            pltpu.VMEM((PACKS * PACKS, 4, LANES), F32),
            pltpu.VMEM((3, 8, THIRD_PAD), jnp.int32),
            dma((6,)),
            dma((2,)),
            dma((8,)),
            dma((8,)),
            dma,
            dma((16,)),
            dma((16,)),
            dma((16,)),
            dma((16,)),
            dma((3,)),
            dma((192,)),
            dma,
            dma,
        ],
        compiler_params=pltpu.CompilerParams(
            collective_id=0, has_side_effects=True, vmem_limit_bytes=60 * 1024 * 1024
        ),
        cost_estimate=pl.CostEstimate(
            flops=4 * LIVE_ROWS * VOCAB_DEV * WIDTH,
            bytes_accessed=4 * VOCAB_DEV * WIDTH,
            transcendentals=2 * LIVE_ROWS * VOCAB_DEV,
        ),
    )(
        gen_hidden,
        gen_gain.reshape(BLOCKS, LANES),
        gen_head,
        dom_hidden,
        dom_gain.reshape(BLOCKS, LANES),
        dom_head,
        targets.reshape(PACKS, LANES),
        docs,
    )
    token, score = pl.pallas_call(
        finish,
        out_shape=(
            jax.ShapeDtypeStruct((1, PACK_ROWS), F32),
            jax.ShapeDtypeStruct((1, DOC_PACK), F32),
        ),
    )(total, docs)
    return token.reshape(PACK_ROWS), score.reshape(DOC_PACK)


def solution(mesh):
    in_specs = (
        P(("dp", "dom"), "gen"),
        P("dp"),
        P(("dp", "gen", "dom"), None),
        P(("dp", "gen"), "dom"),
        P("dp"),
        P(("dp", "gen", "dom"), None),
        P("dp"),
        P("dp"),
    )
    out_specs = (P(("dp", "dom")), P(("dp", "dom")))
    return jax.shard_map(
        per_device, mesh=mesh, in_specs=in_specs, out_specs=out_specs, check_vma=False
    )
```

```python
import jax
import jax.numpy as jnp
from jax import lax
from jax.experimental import pallas as pl
from jax.experimental.pallas import tpu as pltpu
from jax.sharding import PartitionSpec as P

MESH = pl.DeviceIdType.MESH
F32 = jnp.float32
BF16 = jnp.bfloat16

PACKS = 8
PACK_ROWS = 128
DOC_PACK = 8
WIDTH = 4096
VOCAB_DEV = 1024
LANES = 128
BLOCKS = WIDTH // LANES
LIVE_ROWS = 544
THIRD_ROWS = (192, 176, 176)
THIRD_BASE = (0, 192, 368)
THIRD_PAD = 256
AXES = ((0, 1, 2), (1, 2, 0), (2, 0, 1))


def turn(q):
    return q + q // 2 - 2 * (q // 3)


LAYER_HALF = (0, 0, 1, 0, 1, 1, 0, 1)
LAYER_LAST = (0, 3, 0, 1, 3, 1, 2, 2)
CHUNKS = ((0, 1), (1, 3), (4, 4), (8, 4), (12, 4))
SENT_AT = {3: 0, 4: 1}
RELAYED_AT = (0, 0, 2, 3, 4)


def pick(table, k):
    value = jnp.int32(table[0])
    for i in range(1, len(table)):
        if table[i] != table[i - 1]:
            value = jnp.where(k >= i, jnp.int32(table[i]), value)
    return value


def device_of(x, y, z):
    return {"gen": (y // 2) * 4 + x, "dom": z * 2 + y % 2}


def slot_of(x, y, z):
    g, d = (y // 2) * 4 + x, z * 2 + y % 2
    odd = (x + y) % 2
    return (1 - odd) * (g * 4 + z) + odd * (BLOCKS + d * 4 + g // 2)


def remote(src, dst, send_sem, recv_sem, device):
    return pltpu.make_async_remote_copy(
        src_ref=src,
        dst_ref=dst,
        send_sem=send_sem,
        recv_sem=recv_sem,
        device_id=device,
        device_id_type=MESH,
    )


def kernel(
    gen_hidden,
    gen_gain,
    gen_head,
    dom_hidden,
    dom_gain,
    dom_head,
    targets,
    doc_ids,
    total_out,
    heads,
    x0,
    x1,
    x2,
    logits,
    place,
    stage,
    hidden,
    gains,
    ids,
    square_in,
    square_full,
    square_src,
    square_src_full,
    scale_parts,
    scales,
    stats_src,
    stats_in,
    want,
    target_parts,
    load_sem,
    head_sem,
    stage_send,
    stage_recv,
    local_sem,
    square_send,
    square_recv,
    full_send,
    full_recv,
    ring_send,
    ring_recv,
    stats_send,
    stats_recv,
):
    thirds = (x0, x1, x2)
    g, d = lax.axis_index("gen"), lax.axis_index("dom")
    core = lax.axis_index("dp")
    sign = 1 - 2 * core
    x, y, z = g % 4, (g // 4) * 2 + d % 2, d // 2
    here = (x, y, z)
    is_dom = (x + y) % 2

    barrier = pltpu.get_barrier_semaphore()
    for step in range(1, PACKS):
        pl.semaphore_signal(
            barrier, inc=1, device_id={"gen": (g + step) % PACKS}, device_id_type=MESH
        )
        pl.semaphore_signal(
            barrier, inc=1, device_id={"dom": (d + step) % PACKS}, device_id_type=MESH
        )
    pl.semaphore_signal(
        barrier,
        inc=1,
        device_id={"gen": (g + 4) % PACKS, "dom": d + 1 - 2 * (d % 2)},
        device_id_type=MESH,
    )

    loads = [
        pltpu.make_async_copy(gen_hidden, hidden.at[0], load_sem.at[0]),
        pltpu.make_async_copy(dom_hidden, hidden.at[1], load_sem.at[1]),
        pltpu.make_async_copy(gen_gain, gains.at[0], load_sem.at[2]),
        pltpu.make_async_copy(dom_gain, gains.at[1], load_sem.at[3]),
        pltpu.make_async_copy(targets, ids.at[0], load_sem.at[4]),
        pltpu.make_async_copy(doc_ids, ids.at[1], load_sem.at[5]),
    ]
    for load in loads:
        load.start()

    pl.semaphore_wait(barrier, 2 * (PACKS - 1) + 1)

    gen_targets = [2 * q + g % 2 for q in range(4)]
    dom_targets = [2 * q + (d + 1) % 2 for q in range(4)]

    def stage_copy(q, model):
        cols = pl.ds(q * LANES, LANES)
        if model == 0:
            src, row, device = gen_hidden.at[:, cols], d, {"dom": gen_targets[q]}
        else:
            src, row, device = dom_hidden.at[:, cols], g, {"gen": dom_targets[q]}
        far = remote(
            src, stage.at[row], stage_send.at[model * 4 + q], stage_recv.at[row], device
        )
        near = pltpu.make_async_copy(src, stage.at[row], local_sem)
        return far, near

    def targets_self(q, model):
        return gen_targets[q] == d if model == 0 else dom_targets[q] == g

    def each_stage(act_far, act_near):
        for model in range(2):
            for q in range(4):
                mine = targets_self(q, model)
                far, near = stage_copy(q, model)
                if act_near is not None:
                    pl.when(mine)(lambda near=near: act_near(near))
                pl.when(jnp.logical_not(mine))(lambda far=far: act_far(far))

    each_stage(lambda c: c.start(), lambda c: c.start())

    loads[0].wait()
    loads[1].wait()
    for model in range(2):
        total = jnp.zeros((PACK_ROWS, LANES), F32)
        for q in range(4):
            part = hidden[model, :, q * LANES : (q + 1) * LANES].astype(F32)
            total = total + part * part
        row = jnp.sum(total.T, axis=0, keepdims=True)
        square_src[model] = row
        if model == 0:
            square_in[pl.ds(g, 1)] = row[None]
        else:
            square_in[pl.ds(PACKS + d, 1)] = row[None]

    def square_copy(step, model):
        if model == 0:
            device, own, other = {"gen": (g + step) % PACKS}, g, (g + PACKS - step) % PACKS
        else:
            device = {"dom": (d + step) % PACKS}
            own, other = PACKS + d, PACKS + (d + PACKS - step) % PACKS
        send = square_send.at[model * PACKS + step]
        out = remote(
            square_src.at[model], square_in.at[own], send, square_recv.at[own], device
        )
        arrival = remote(
            square_src.at[model], square_in.at[other], send, square_recv.at[other], device
        )
        return out, arrival

    for step in range(1, PACKS):
        for model in range(2):
            square_copy(step, model)[0].start()

    for load in loads[2:]:
        load.wait()
    docs = ids[1]
    counts = jnp.sum((docs >= 0).astype(jnp.int32), axis=1, keepdims=True)
    lane = lax.broadcasted_iota(jnp.int32, (THIRD_PAD, LANES), 1)
    sub = lax.broadcasted_iota(jnp.int32, (THIRD_PAD, LANES), 0)
    offset = jnp.zeros((1, 1), jnp.int32)
    for p in range(PACKS):
        count = counts[p : p + 1, :]
        for t in range(3):
            hit = jnp.logical_and(sub + (THIRD_BASE[t] - offset) == lane, lane < count)
            hit = jnp.logical_and(hit, sub < THIRD_ROWS[t])
            place[t, :, p * LANES : (p + 1) * LANES] = jnp.where(hit, 1.0, 0.0).astype(BF16)
        offset = offset + count

    def source(p):
        return jnp.where(is_dom == 1, g, d) == p

    for p in range(PACKS):
        mine = source(p)

        @pl.when(jnp.logical_not(mine))
        def _(p=p):
            remote(
                stage.at[p], stage.at[p], stage_send.at[0], stage_recv.at[p], {"dom": d}
            ).wait_recv()

        @pl.when(mine)
        def _(p=p):
            pltpu.make_async_copy(stage.at[p], stage.at[p], local_sem).wait()

    for t in range(3):
        rows = jnp.dot(
            place[t],
            stage[...].reshape(PACKS * PACK_ROWS, LANES),
            preferred_element_type=F32,
        ).astype(BF16)
        thirds[t][0] = rows

    def moved(axis, by):
        at = list(here)
        at[axis] = (at[axis] + by + 4) % 4
        return device_of(*at)

    ahead = [moved(axis, sign) for axis in range(3)]
    behind = [moved(axis, -sign) for axis in range(3)]

    def block_at(t, n, last):
        at = list(here)
        for k, u in enumerate((turn(n % 4), turn(n // 4), last)):
            axis = AXES[t][k]
            at[axis] = (at[axis] - sign * u + 4) % 4
        return slot_of(*at)

    def rows_of(t, slot, count):
        return thirds[t].at[pl.ds(slot, count), pl.ds(0, THIRD_ROWS[t])]

    def push(t, k, forward, src, dst, count=1):
        device = (ahead if forward else behind)[AXES[t][k]]
        remote(
            rows_of(t, src, count),
            rows_of(t, dst, count),
            ring_send.at[t],
            ring_recv.at[t * 64 + dst],
            device,
        ).start()

    def arrived(t, dst, count=1):
        ref = rows_of(t, dst, count)
        remote(ref, ref, ring_send.at[t], ring_recv.at[t * 64 + dst], ahead[0]).wait_recv()

    def push_second(t, n):
        push(t, 1, True, n, 4 + n)
        push(t, 1, False, n, 8 + n)

    def announce(t, c):
        first, count = CHUNKS[c]
        push(t, 2, True, first, 16 + first, count)
        push(t, 2, False, first, 48 + first, count)

    def relay(t, c):
        first, count = CHUNKS[c]
        arrived(t, 16 + first, count)
        push(t, 2, True, 16 + first, 32 + first, count)

    for t in range(3):
        push(t, 0, True, 0, 1)
        push(t, 0, False, 0, 2)
    for t in range(3):
        push_second(t, 0)
    for t in range(3):
        announce(t, 0)

    def load_heads(k, carry):
        cols = pl.ds(pl.multiple_of(k * LANES, LANES), LANES)
        pltpu.make_async_copy(gen_head.at[:, cols], heads.at[0, k], head_sem.at[0]).start()
        pltpu.make_async_copy(dom_head.at[:, cols], heads.at[1, k], head_sem.at[1]).start()
        return carry

    lax.fori_loop(0, BLOCKS, load_heads, 0)

    def first_axis(n):
        for t in range(3):
            arrived(t, n)
            if n == 1:
                push(t, 0, True, 1, 3)
            push_second(t, n)

    first_axis(1)

    for step in range(1, PACKS):
        for model in range(2):
            square_copy(step, model)[1].wait_recv()
    for model in range(2):
        row = jnp.sum(square_in[model * PACKS : (model + 1) * PACKS], axis=0)
        square_src_full[model] = row
        own = d if model == 0 else PACKS + g
        square_full[pl.ds(own, 1)] = row[None]

    def full_copy(step, model):
        back = PACKS - step
        if model == 0:
            device, own, other = {"dom": (d + step) % PACKS}, d, (d + back) % PACKS
        else:
            device = {"gen": (g + step) % PACKS}
            own, other = PACKS + g, PACKS + (g + back) % PACKS
        src, send = square_src_full.at[model], full_send.at[model * PACKS + step]
        out = remote(src, square_full.at[own], send, full_recv.at[own], device)
        arrival = remote(src, square_full.at[other], send, full_recv.at[other], device)
        return out, arrival

    for step in range(1, PACKS):
        for model in range(2):
            full_copy(step, model)[0].start()

    first_axis(2)

    def clear(slot, carry):
        for t in range(3):
            pad = THIRD_PAD - THIRD_ROWS[t]
            thirds[t][pl.ds(slot, 1), THIRD_ROWS[t] :, :] = jnp.zeros((1, pad, LANES), BF16)
        return carry

    lax.fori_loop(0, 2 * BLOCKS, clear, 0)

    def clear_logits(i, carry):
        rows = pl.ds(pl.multiple_of(i * 64, 64), 64)
        for a in range(6):
            logits[a, rows, :] = jnp.zeros((64, THIRD_PAD), F32)
        return carry

    lax.fori_loop(0, VOCAB_DEV // 64, clear_logits, 0)

    first_axis(3)
    for t in range(3):
        announce(t, 1)

    first_column = (g * PACKS + d) * VOCAB_DEV
    tgt = ids[0]
    high, low = tgt // 256, tgt % 256
    rows = lax.broadcasted_iota(jnp.int32, (32, LANES), 0)
    for p in range(PACKS):
        pair = jnp.where(
            rows < 16,
            jnp.broadcast_to(high[p : p + 1, :], (32, LANES)),
            jnp.broadcast_to(low[p : p + 1, :], (32, LANES)),
        )
        target_parts[:, p * LANES : (p + 1) * LANES] = pair.astype(F32).astype(BF16)
    for t in range(3):
        got = lax.dot_general(
            target_parts[...], place[t], (((1,), (1,)), ((), ())), preferred_element_type=F32
        )
        column = (got[0:8] * 256.0 + got[16:24]).astype(jnp.int32) - first_column
        want[t] = column

    for n in range(4):
        for t in range(3):
            arrived(t, 4 + n)
            push(t, 1, True, 4 + n, 12 + n)
    for t in range(3):
        announce(t, 2)

    def add_layer(t, half, last):
        slots = [last * 16 + 8 * half + i for i in range(8)]
        blocks = [block_at(t, 8 * half + i, last) for i in range(8)]
        if t == 0:
            order = (0, 3, 5, 6, 1, 2, 4, 7)
        elif t == 1:
            order = (0, 3, 4, 7, 1, 2, 5, 6)
        else:
            order = (0, 1, 2, 3, 4, 5, 6, 7)
        for group in (order[:4], order[4:]):
            model = blocks[group[0]] // BLOCKS
            part = [blocks[i] % BLOCKS for i in group]
            left = jnp.concatenate([heads[model, b] for b in part], axis=1)
            scale = scales[2 * t + model]
            right = jnp.concatenate(
                [
                    (
                        thirds[t][slots[i]].astype(F32) * scale * gains[model, pl.ds(b, 1), :]
                    ).astype(BF16)
                    for i, b in zip(group, part)
                ],
                axis=1,
            )
            logits[2 * t + model] += lax.dot_general(
                left, right, (((1,), (1,)), ((), ())), preferred_element_type=F32
            )

    for step in range(1, PACKS):
        for model in range(2):
            full_copy(step, model)[1].wait_recv()
    for model in range(2):
        for p in range(PACKS):
            rest = lax.rsqrt(square_full[model * PACKS + p] / WIDTH + 1e-05)
            rest = jnp.broadcast_to(rest, (PACK_ROWS, LANES)).T
            for part in range(3):
                head = rest.astype(BF16)
                scale_parts[part, p * PACK_ROWS : (p + 1) * PACK_ROWS, :] = head
                rest = rest - head.astype(F32)
        for t in range(3):
            total = jnp.zeros((THIRD_PAD, LANES), F32)
            for part in range(3):
                total = total + jnp.dot(
                    place[t], scale_parts[part], preferred_element_type=F32
                )
            scales[2 * t + model] = total

    pltpu.make_async_copy(heads.at[0], heads.at[0], head_sem.at[0]).wait()
    pltpu.make_async_copy(heads.at[1], heads.at[1], head_sem.at[1]).wait()

    def layer(k, carry):
        half, last = pick(LAYER_HALF, k), pick(LAYER_LAST, k)
        for t in range(3):

            for c in (3, 4):

                @pl.when(k == SENT_AT[c])
                def _(t=t, c=c):
                    for n in range(CHUNKS[c][0], CHUNKS[c][0] + CHUNKS[c][1]):
                        arrived(t, n)
                    announce(t, c)

            for c in range(5):
                pl.when(k == RELAYED_AT[c])(lambda t=t, c=c: relay(t, c))
            for h, held in enumerate(((0, 1, 2), (3, 4))):

                @pl.when((last >= 2) & (half == h))
                def _(t=t, held=held):
                    for c in held:
                        arrived(t, last * 16 + CHUNKS[c][0], CHUNKS[c][1])

            add_layer(t, half, last)

        return carry

    lax.fori_loop(0, 8, layer, 0)

    CHUNK = 64
    steps = VOCAB_DEV // CHUNK
    spread = jnp.zeros((32, VOCAB_DEV), F32)
    for t in range(3):

        def highest(i, so_far, t=t):
            rows = pl.ds(pl.multiple_of(i * CHUNK, CHUNK), CHUNK)
            out = []
            for model in range(2):
                block = logits[2 * t + model, rows, :].reshape(CHUNK // 8, 8, THIRD_PAD)
                out.append(jnp.maximum(so_far[model], jnp.max(block, axis=0)))
            return tuple(out)

        least = jnp.full((8, THIRD_PAD), -jnp.inf, F32)
        tops = lax.fori_loop(0, steps, highest, (least, least))
        tops = [jnp.max(top, axis=0, keepdims=True) for top in tops]
        wanted = want[t]

        def totals(i, so_far, t=t, tops=tops, wanted=wanted):
            rows = pl.ds(pl.multiple_of(i * CHUNK, CHUNK), CHUNK)
            gen = logits[2 * t, rows, :].reshape(CHUNK // 8, 8, THIRD_PAD)
            dom = logits[2 * t + 1, rows, :].reshape(CHUNK // 8, 8, THIRD_PAD)
            gen_sum = so_far[0] + jnp.sum(jnp.exp(gen - tops[0][None]), axis=0)
            dom_sum = so_far[1] + jnp.sum(jnp.exp(dom - tops[1][None]), axis=0)
            entry = (
                lax.broadcasted_iota(jnp.int32, (CHUNK // 8, 8, THIRD_PAD), 0) * 8
                + lax.broadcasted_iota(jnp.int32, (CHUNK // 8, 8, THIRD_PAD), 1)
                + i * CHUNK
            )
            picked = so_far[2] + jnp.sum(
                jnp.where(entry == wanted[None], dom - gen, 0.0), axis=0
            )
            return gen_sum, dom_sum, picked

        zero = jnp.zeros((8, THIRD_PAD), F32)
        sums = lax.fori_loop(0, steps, totals, (zero, zero, zero))
        sums = [jnp.sum(value, axis=0, keepdims=True) for value in sums]
        values = [tops[0] + jnp.log(sums[0]), tops[1] + jnp.log(sums[1]), sums[2]]
        row = lax.broadcasted_iota(jnp.int32, (32, THIRD_PAD), 0)
        stack = jnp.zeros((32, THIRD_PAD), F32)
        for k in range(3):
            rest = values[k]
            for part in range(3):
                head = rest.astype(BF16).astype(F32)
                stack = jnp.where(row == part * 8 + k, head, stack)
                rest = rest - head
        spread = spread + jnp.dot(stack.astype(BF16), place[t], preferred_element_type=F32)
    spread = spread[0:8] + spread[8:16] + spread[16:24]
    for p in range(PACKS):
        stats_src[p] = spread[0:4, p * LANES : (p + 1) * LANES]

    me = g * PACKS + d

    def share(step, carry):
        peer = (me + step) % (PACKS * PACKS)
        remote(
            stats_src.at[peer % PACKS],
            stats_in.at[me],
            stats_send,
            stats_recv,
            {"gen": peer // PACKS, "dom": peer % PACKS},
        ).start()
        return carry

    lax.fori_loop(1, PACKS * PACKS, share, 0)
    stats_in[pl.ds(me, 1)] = stats_src[pl.ds(d, 1)]

    each_stage(lambda c: c.wait_send(), None)
    for step in range(1, PACKS):
        for model in range(2):
            square_copy(step, model)[0].wait_send()
            full_copy(step, model)[0].wait_send()
    for t in range(3):
        ref = thirds[t].at[pl.ds(0, 63), pl.ds(0, THIRD_ROWS[t])]
        remote(ref, ref, ring_send.at[t], ring_recv.at[0], ahead[0]).wait_send()

    others = stats_in.at[pl.ds(0, PACKS * PACKS - 1)]
    remote(others, others, stats_send, stats_recv, ahead[0]).wait()
    block = stats_in[...]
    top = jnp.max(block, axis=0)
    total = top + jnp.log(jnp.sum(jnp.exp(block - top[None]), axis=0))
    row = lax.broadcasted_iota(jnp.int32, (4, LANES), 0)
    total_out[...] = jnp.where(row < 2, total, jnp.sum(block, axis=0))


def finish(total, doc_ids, token_out, score_out):
    d = lax.axis_index("dom")
    token = total[2:3, :] - total[1:2, :] + total[0:1, :]
    own_docs = doc_ids[pl.ds(d, 1), :]
    token = jnp.where(own_docs >= 0, token, 0.0)
    token_out[...] = token
    row = lax.broadcasted_iota(jnp.int32, (DOC_PACK, LANES), 0)
    col = lax.broadcasted_iota(jnp.int32, (DOC_PACK, LANES), 1)
    member = (own_docs - d * DOC_PACK) == row
    doc_sum = jnp.sum(jnp.where(member, token, 0.0), axis=1, keepdims=True)
    doc_count = jnp.sum(jnp.where(member, 1.0, 0.0), axis=1, keepdims=True)
    score = jnp.sum(jnp.where(row == col, doc_sum / doc_count, 0.0), axis=0, keepdims=True)
    score_out[...] = score[:, :DOC_PACK]


def per_device(gen_hidden, gen_gain, gen_head, dom_hidden, dom_gain, dom_head, targets, doc_ids):
    anywhere = pl.BlockSpec(memory_space=pl.ANY)
    dma = pltpu.SemaphoreType.DMA
    slots = pltpu.VMEM((2 * BLOCKS, THIRD_PAD, LANES), BF16)
    docs = doc_ids.reshape(PACKS, LANES)
    total = pl.pallas_call(
        kernel,
        out_shape=jax.ShapeDtypeStruct((4, LANES), F32),
        in_specs=[anywhere] * 8,
        out_specs=pl.BlockSpec(memory_space=pltpu.VMEM),
        scratch_shapes=[
            pltpu.VMEM((2, BLOCKS, VOCAB_DEV, LANES), BF16),
            slots,
            slots,
            slots,
            pltpu.VMEM((6, VOCAB_DEV, THIRD_PAD), F32),
            pltpu.VMEM((3, THIRD_PAD, PACKS * PACK_ROWS), BF16),
            pltpu.VMEM((PACKS, PACK_ROWS, LANES), BF16),
            pltpu.VMEM((2, PACK_ROWS, 4 * LANES), BF16),
            pltpu.VMEM((2, BLOCKS, LANES), F32),
            pltpu.VMEM((2, PACKS, LANES), jnp.int32),
            pltpu.VMEM((2 * PACKS, 1, LANES), F32),
            pltpu.VMEM((2 * PACKS, 1, LANES), F32),
            pltpu.VMEM((2, 1, LANES), F32),
            pltpu.VMEM((2, 1, LANES), F32),
            pltpu.VMEM((3, PACKS * PACK_ROWS, LANES), BF16),
            pltpu.VMEM((6, THIRD_PAD, LANES), F32),
            pltpu.VMEM((PACKS, 4, LANES), F32),
            pltpu.VMEM((PACKS * PACKS, 4, LANES), F32),
            pltpu.VMEM((3, 8, THIRD_PAD), jnp.int32),
            pltpu.VMEM((32, PACKS * PACK_ROWS), BF16),
            dma((6,)),
            dma((2,)),
            dma((8,)),
            dma((8,)),
            dma,
            dma((16,)),
            dma((16,)),
            dma((16,)),
            dma((16,)),
            dma((3,)),
            dma((192,)),
            dma,
            dma,
        ],
        compiler_params=pltpu.CompilerParams(
            collective_id=0, has_side_effects=True, vmem_limit_bytes=60 * 1024 * 1024
        ),
        cost_estimate=pl.CostEstimate(
            flops=4 * LIVE_ROWS * VOCAB_DEV * WIDTH,
            bytes_accessed=4 * VOCAB_DEV * WIDTH,
            transcendentals=2 * LIVE_ROWS * VOCAB_DEV,
        ),
    )(
        gen_hidden,
        gen_gain.reshape(BLOCKS, LANES),
        gen_head,
        dom_hidden,
        dom_gain.reshape(BLOCKS, LANES),
        dom_head,
        targets.reshape(PACKS, LANES),
        docs,
    )
    token, score = pl.pallas_call(
        finish,
        out_shape=(
            jax.ShapeDtypeStruct((1, PACK_ROWS), F32),
            jax.ShapeDtypeStruct((1, DOC_PACK), F32),
        ),
    )(total, docs)
    return token.reshape(PACK_ROWS), score.reshape(DOC_PACK)


def solution(mesh):
    in_specs = (
        P(("dp", "dom"), "gen"),
        P("dp"),
        P(("dp", "gen", "dom"), None),
        P(("dp", "gen"), "dom"),
        P("dp"),
        P(("dp", "gen", "dom"), None),
        P("dp"),
        P("dp"),
    )
    out_specs = (P(("dp", "dom")), P(("dp", "dom")))
    return jax.shard_map(
        per_device, mesh=mesh, in_specs=in_specs, out_specs=out_specs, check_vma=False
    )
```

```python
import jax
import jax.numpy as jnp
from jax import lax
from jax.experimental import pallas as pl
from jax.experimental.pallas import tpu as pltpu
from jax.sharding import PartitionSpec as P

MESH = pl.DeviceIdType.MESH
F32 = jnp.float32
BF16 = jnp.bfloat16

PACKS = 8
PACK_ROWS = 128
DOC_PACK = 8
WIDTH = 4096
VOCAB_DEV = 1024
LANES = 128
BLOCKS = WIDTH // LANES
LIVE_ROWS = 544
THIRD_ROWS = (192, 176, 176)
THIRD_BASE = (0, 192, 368)
THIRD_PAD = 256
AXES = ((0, 1, 2), (1, 2, 0), (2, 0, 1))


def turn(q):
    return q + q // 2 - 2 * (q // 3)


LAYER_HALF = (0, 0, 1, 0, 1, 1, 0, 1)
LAYER_LAST = (0, 3, 0, 1, 3, 1, 2, 2)
CHUNKS = ((0, 1), (1, 3), (4, 4), (8, 4), (12, 4))
SENT_AT = {3: 0, 4: 1}
RELAYED_AT = (0, 1, 2, 3, 4)


def pick(table, k):
    value = jnp.int32(table[0])
    for i in range(1, len(table)):
        if table[i] != table[i - 1]:
            value = jnp.where(k >= i, jnp.int32(table[i]), value)
    return value


def device_of(x, y, z):
    return {"gen": (y // 2) * 4 + x, "dom": z * 2 + y % 2}


def slot_of(x, y, z):
    g, d = (y // 2) * 4 + x, z * 2 + y % 2
    odd = (x + y) % 2
    return (1 - odd) * (g * 4 + z) + odd * (BLOCKS + d * 4 + g // 2)


def remote(src, dst, send_sem, recv_sem, device):
    return pltpu.make_async_remote_copy(
        src_ref=src,
        dst_ref=dst,
        send_sem=send_sem,
        recv_sem=recv_sem,
        device_id=device,
        device_id_type=MESH,
    )


def kernel(
    gen_hidden,
    gen_gain,
    gen_head,
    dom_hidden,
    dom_gain,
    dom_head,
    targets,
    doc_ids,
    total_out,
    heads,
    x0,
    x1,
    x2,
    logits,
    place,
    stage,
    hidden,
    gains,
    ids,
    square_in,
    square_full,
    square_src,
    square_src_full,
    scale_parts,
    scales,
    stats_src,
    stats_in,
    want,
    target_parts,
    load_sem,
    head_sem,
    stage_send,
    stage_recv,
    local_sem,
    square_send,
    square_recv,
    full_send,
    full_recv,
    ring_send,
    ring_recv,
    stats_send,
    stats_recv,
):
    thirds = (x0, x1, x2)
    g, d = lax.axis_index("gen"), lax.axis_index("dom")
    core = lax.axis_index("dp")
    sign = 1 - 2 * core
    x, y, z = g % 4, (g // 4) * 2 + d % 2, d // 2
    here = (x, y, z)
    is_dom = (x + y) % 2

    barrier = pltpu.get_barrier_semaphore()
    for step in range(1, PACKS):
        pl.semaphore_signal(
            barrier, inc=1, device_id={"gen": (g + step) % PACKS}, device_id_type=MESH
        )
        pl.semaphore_signal(
            barrier, inc=1, device_id={"dom": (d + step) % PACKS}, device_id_type=MESH
        )
    pl.semaphore_signal(
        barrier,
        inc=1,
        device_id={"gen": (g + 4) % PACKS, "dom": d + 1 - 2 * (d % 2)},
        device_id_type=MESH,
    )

    loads = [
        pltpu.make_async_copy(gen_hidden, hidden.at[0], load_sem.at[0]),
        pltpu.make_async_copy(dom_hidden, hidden.at[1], load_sem.at[1]),
        pltpu.make_async_copy(gen_gain, gains.at[0], load_sem.at[2]),
        pltpu.make_async_copy(dom_gain, gains.at[1], load_sem.at[3]),
        pltpu.make_async_copy(targets, ids.at[0], load_sem.at[4]),
        pltpu.make_async_copy(doc_ids, ids.at[1], load_sem.at[5]),
    ]
    for load in loads:
        load.start()

    pl.semaphore_wait(barrier, 2 * (PACKS - 1) + 1)

    gen_targets = [2 * q + g % 2 for q in range(4)]
    dom_targets = [2 * q + (d + 1) % 2 for q in range(4)]

    def stage_copy(q, model):
        cols = pl.ds(q * LANES, LANES)
        if model == 0:
            src, row, device = gen_hidden.at[:, cols], d, {"dom": gen_targets[q]}
        else:
            src, row, device = dom_hidden.at[:, cols], g, {"gen": dom_targets[q]}
        far = remote(
            src, stage.at[row], stage_send.at[model * 4 + q], stage_recv.at[row], device
        )
        near = pltpu.make_async_copy(src, stage.at[row], local_sem)
        return far, near

    def targets_self(q, model):
        return gen_targets[q] == d if model == 0 else dom_targets[q] == g

    def each_stage(act_far, act_near):
        for model in range(2):
            for q in range(4):
                mine = targets_self(q, model)
                far, near = stage_copy(q, model)
                if act_near is not None:
                    pl.when(mine)(lambda near=near: act_near(near))
                pl.when(jnp.logical_not(mine))(lambda far=far: act_far(far))

    each_stage(lambda c: c.start(), lambda c: c.start())

    loads[0].wait()
    loads[1].wait()
    for model in range(2):
        total = jnp.zeros((PACK_ROWS, LANES), F32)
        for q in range(4):
            part = hidden[model, :, q * LANES : (q + 1) * LANES].astype(F32)
            total = total + part * part
        row = jnp.sum(total.T, axis=0, keepdims=True)
        square_src[model] = row
        if model == 0:
            square_in[pl.ds(g, 1)] = row[None]
        else:
            square_in[pl.ds(PACKS + d, 1)] = row[None]

    def square_copy(step, model):
        if model == 0:
            device, own, other = {"gen": (g + step) % PACKS}, g, (g + PACKS - step) % PACKS
        else:
            device = {"dom": (d + step) % PACKS}
            own, other = PACKS + d, PACKS + (d + PACKS - step) % PACKS
        send = square_send.at[model * PACKS + step]
        out = remote(
            square_src.at[model], square_in.at[own], send, square_recv.at[own], device
        )
        arrival = remote(
            square_src.at[model], square_in.at[other], send, square_recv.at[other], device
        )
        return out, arrival

    for step in range(1, PACKS):
        for model in range(2):
            square_copy(step, model)[0].start()

    for load in loads[2:]:
        load.wait()
    docs = ids[1]
    counts = jnp.sum((docs >= 0).astype(jnp.int32), axis=1, keepdims=True)
    lane = lax.broadcasted_iota(jnp.int32, (THIRD_PAD, LANES), 1)
    sub = lax.broadcasted_iota(jnp.int32, (THIRD_PAD, LANES), 0)
    offset = jnp.zeros((1, 1), jnp.int32)
    for p in range(PACKS):
        count = counts[p : p + 1, :]
        for t in range(3):
            hit = jnp.logical_and(sub + (THIRD_BASE[t] - offset) == lane, lane < count)
            hit = jnp.logical_and(hit, sub < THIRD_ROWS[t])
            place[t, :, p * LANES : (p + 1) * LANES] = jnp.where(hit, 1.0, 0.0).astype(BF16)
        offset = offset + count

    def load_heads(k, carry):
        cols = pl.ds(pl.multiple_of(k * LANES, LANES), LANES)
        pltpu.make_async_copy(gen_head.at[:, cols], heads.at[0, k], head_sem.at[0]).start()
        pltpu.make_async_copy(dom_head.at[:, cols], heads.at[1, k], head_sem.at[1]).start()
        return carry

    lax.fori_loop(0, BLOCKS, load_heads, 0)

    def source(p):
        return jnp.where(is_dom == 1, g, d) == p

    for p in range(PACKS):
        mine = source(p)

        @pl.when(jnp.logical_not(mine))
        def _(p=p):
            remote(
                stage.at[p], stage.at[p], stage_send.at[0], stage_recv.at[p], {"dom": d}
            ).wait_recv()

        @pl.when(mine)
        def _(p=p):
            pltpu.make_async_copy(stage.at[p], stage.at[p], local_sem).wait()

    for t in range(3):
        rows = jnp.dot(
            place[t],
            stage[...].reshape(PACKS * PACK_ROWS, LANES),
            preferred_element_type=F32,
        ).astype(BF16)
        thirds[t][0] = rows

    def moved(axis, by):
        at = list(here)
        at[axis] = (at[axis] + by + 4) % 4
        return device_of(*at)

    ahead = [moved(axis, sign) for axis in range(3)]
    behind = [moved(axis, -sign) for axis in range(3)]

    def block_at(t, n, last):
        at = list(here)
        for k, u in enumerate((turn(n % 4), turn(n // 4), last)):
            axis = AXES[t][k]
            at[axis] = (at[axis] - sign * u + 4) % 4
        return slot_of(*at)

    def rows_of(t, slot, count):
        return thirds[t].at[pl.ds(slot, count), pl.ds(0, THIRD_ROWS[t])]

    def push(t, k, forward, src, dst, count=1):
        device = (ahead if forward else behind)[AXES[t][k]]
        remote(
            rows_of(t, src, count),
            rows_of(t, dst, count),
            ring_send.at[t],
            ring_recv.at[t * 64 + dst],
            device,
        ).start()

    def arrived(t, dst, count=1):
        ref = rows_of(t, dst, count)
        remote(ref, ref, ring_send.at[t], ring_recv.at[t * 64 + dst], ahead[0]).wait_recv()

    def push_second(t, n):
        push(t, 1, True, n, 4 + n)
        push(t, 1, False, n, 8 + n)

    def announce(t, c):
        first, count = CHUNKS[c]
        push(t, 2, True, first, 16 + first, count)
        push(t, 2, False, first, 48 + first, count)

    def relay(t, c):
        first, count = CHUNKS[c]
        arrived(t, 16 + first, count)
        push(t, 2, True, 16 + first, 32 + first, count)

    for t in range(3):
        push(t, 0, True, 0, 1)
        push(t, 0, False, 0, 2)
    for t in range(3):
        push_second(t, 0)
    for t in range(3):
        announce(t, 0)

    def first_axis(n):
        for t in range(3):
            arrived(t, n)
            if n == 1:
                push(t, 0, True, 1, 3)
            push_second(t, n)

    first_axis(1)

    for step in range(1, PACKS):
        for model in range(2):
            square_copy(step, model)[1].wait_recv()
    for model in range(2):
        row = jnp.sum(square_in[model * PACKS : (model + 1) * PACKS], axis=0)
        square_src_full[model] = row
        own = d if model == 0 else PACKS + g
        square_full[pl.ds(own, 1)] = row[None]

    def full_copy(step, model):
        back = PACKS - step
        if model == 0:
            device, own, other = {"dom": (d + step) % PACKS}, d, (d + back) % PACKS
        else:
            device = {"gen": (g + step) % PACKS}
            own, other = PACKS + g, PACKS + (g + back) % PACKS
        src, send = square_src_full.at[model], full_send.at[model * PACKS + step]
        out = remote(src, square_full.at[own], send, full_recv.at[own], device)
        arrival = remote(src, square_full.at[other], send, full_recv.at[other], device)
        return out, arrival

    for step in range(1, PACKS):
        for model in range(2):
            full_copy(step, model)[0].start()

    first_axis(2)

    def clear(slot, carry):
        for t in range(3):
            pad = THIRD_PAD - THIRD_ROWS[t]
            thirds[t][pl.ds(slot, 1), THIRD_ROWS[t] :, :] = jnp.zeros((1, pad, LANES), BF16)
        return carry

    lax.fori_loop(0, 2 * BLOCKS, clear, 0)

    def clear_logits(i, carry):
        rows = pl.ds(pl.multiple_of(i * 64, 64), 64)
        for a in range(6):
            logits[a, rows, :] = jnp.zeros((64, THIRD_PAD), F32)
        return carry

    lax.fori_loop(0, VOCAB_DEV // 64, clear_logits, 0)

    first_axis(3)
    for t in range(3):
        announce(t, 1)

    first_column = (g * PACKS + d) * VOCAB_DEV
    tgt = ids[0]
    high, low = tgt // 256, tgt % 256
    rows = lax.broadcasted_iota(jnp.int32, (32, LANES), 0)
    for p in range(PACKS):
        pair = jnp.where(
            rows < 16,
            jnp.broadcast_to(high[p : p + 1, :], (32, LANES)),
            jnp.broadcast_to(low[p : p + 1, :], (32, LANES)),
        )
        target_parts[:, p * LANES : (p + 1) * LANES] = pair.astype(F32).astype(BF16)
    for t in range(3):
        got = lax.dot_general(
            target_parts[...], place[t], (((1,), (1,)), ((), ())), preferred_element_type=F32
        )
        column = (got[0:8] * 256.0 + got[16:24]).astype(jnp.int32) - first_column
        want[t] = column

    for n in range(4):
        for t in range(3):
            arrived(t, 4 + n)
            push(t, 1, True, 4 + n, 12 + n)
    for t in range(3):
        announce(t, 2)

    def add_layer(t, half, last):
        slots = [last * 16 + 8 * half + i for i in range(8)]
        blocks = [block_at(t, 8 * half + i, last) for i in range(8)]
        if t == 0:
            order = (0, 3, 5, 6, 1, 2, 4, 7)
        elif t == 1:
            order = (0, 3, 4, 7, 1, 2, 5, 6)
        else:
            order = (0, 1, 2, 3, 4, 5, 6, 7)
        for group in (order[:4], order[4:]):
            model = blocks[group[0]] // BLOCKS
            part = [blocks[i] % BLOCKS for i in group]
            left = jnp.concatenate([heads[model, b] for b in part], axis=1)
            scale = scales[2 * t + model]
            right = jnp.concatenate(
                [
                    (
                        thirds[t][slots[i]].astype(F32) * scale * gains[model, pl.ds(b, 1), :]
                    ).astype(BF16)
                    for i, b in zip(group, part)
                ],
                axis=1,
            )
            logits[2 * t + model] += lax.dot_general(
                left, right, (((1,), (1,)), ((), ())), preferred_element_type=F32
            )

    for step in range(1, PACKS):
        for model in range(2):
            full_copy(step, model)[1].wait_recv()
    for model in range(2):
        for p in range(PACKS):
            rest = lax.rsqrt(square_full[model * PACKS + p] / WIDTH + 1e-05)
            rest = jnp.broadcast_to(rest, (PACK_ROWS, LANES)).T
            for part in range(3):
                head = rest.astype(BF16)
                scale_parts[part, p * PACK_ROWS : (p + 1) * PACK_ROWS, :] = head
                rest = rest - head.astype(F32)
        for t in range(3):
            total = jnp.zeros((THIRD_PAD, LANES), F32)
            for part in range(3):
                total = total + jnp.dot(
                    place[t], scale_parts[part], preferred_element_type=F32
                )
            scales[2 * t + model] = total

    pltpu.make_async_copy(heads.at[0], heads.at[0], head_sem.at[0]).wait()
    pltpu.make_async_copy(heads.at[1], heads.at[1], head_sem.at[1]).wait()

    def layer(k, carry):
        half, last = pick(LAYER_HALF, k), pick(LAYER_LAST, k)
        for t in range(3):

            for c in (3, 4):

                @pl.when(k == SENT_AT[c])
                def _(t=t, c=c):
                    for n in range(CHUNKS[c][0], CHUNKS[c][0] + CHUNKS[c][1]):
                        arrived(t, n)
                    announce(t, c)

            for c in range(5):
                pl.when(k == RELAYED_AT[c])(lambda t=t, c=c: relay(t, c))
            for h, held in enumerate(((0, 1, 2), (3, 4))):

                @pl.when((last >= 2) & (half == h))
                def _(t=t, held=held):
                    for c in held:
                        arrived(t, last * 16 + CHUNKS[c][0], CHUNKS[c][1])

            add_layer(t, half, last)

        return carry

    lax.fori_loop(0, 8, layer, 0)

    CHUNK = 128
    steps = VOCAB_DEV // CHUNK
    spread = jnp.zeros((32, VOCAB_DEV), F32)
    for t in range(3):

        def highest(i, so_far, t=t):
            rows = pl.ds(pl.multiple_of(i * CHUNK, CHUNK), CHUNK)
            out = []
            for model in range(2):
                block = logits[2 * t + model, rows, :].reshape(CHUNK // 8, 8, THIRD_PAD)
                out.append(jnp.maximum(so_far[model], jnp.max(block, axis=0)))
            return tuple(out)

        least = jnp.full((8, THIRD_PAD), -jnp.inf, F32)
        tops = lax.fori_loop(0, steps, highest, (least, least))
        tops = [jnp.max(top, axis=0, keepdims=True) for top in tops]
        wanted = want[t]

        def totals(i, so_far, t=t, tops=tops, wanted=wanted):
            rows = pl.ds(pl.multiple_of(i * CHUNK, CHUNK), CHUNK)
            gen = logits[2 * t, rows, :].reshape(CHUNK // 8, 8, THIRD_PAD)
            dom = logits[2 * t + 1, rows, :].reshape(CHUNK // 8, 8, THIRD_PAD)
            gen_sum = so_far[0] + jnp.sum(jnp.exp(gen - tops[0][None]), axis=0)
            dom_sum = so_far[1] + jnp.sum(jnp.exp(dom - tops[1][None]), axis=0)
            entry = (
                lax.broadcasted_iota(jnp.int32, (CHUNK // 8, 8, THIRD_PAD), 0) * 8
                + lax.broadcasted_iota(jnp.int32, (CHUNK // 8, 8, THIRD_PAD), 1)
                + i * CHUNK
            )
            picked = so_far[2] + jnp.sum(
                jnp.where(entry == wanted[None], dom - gen, 0.0), axis=0
            )
            return gen_sum, dom_sum, picked

        zero = jnp.zeros((8, THIRD_PAD), F32)
        sums = lax.fori_loop(0, steps, totals, (zero, zero, zero))
        sums = [jnp.sum(value, axis=0, keepdims=True) for value in sums]
        values = [tops[0] + jnp.log(sums[0]), tops[1] + jnp.log(sums[1]), sums[2]]
        row = lax.broadcasted_iota(jnp.int32, (32, THIRD_PAD), 0)
        stack = jnp.zeros((32, THIRD_PAD), F32)
        for k in range(3):
            rest = values[k]
            for part in range(3):
                head = rest.astype(BF16).astype(F32)
                stack = jnp.where(row == part * 8 + k, head, stack)
                rest = rest - head
        spread = spread + jnp.dot(stack.astype(BF16), place[t], preferred_element_type=F32)
    spread = spread[0:8] + spread[8:16] + spread[16:24]
    for p in range(PACKS):
        stats_src[p] = spread[0:4, p * LANES : (p + 1) * LANES]

    me = g * PACKS + d

    def share(step, carry):
        peer = (me + step) % (PACKS * PACKS)
        remote(
            stats_src.at[peer % PACKS],
            stats_in.at[me],
            stats_send,
            stats_recv,
            {"gen": peer // PACKS, "dom": peer % PACKS},
        ).start()
        return carry

    lax.fori_loop(1, PACKS * PACKS, share, 0)
    stats_in[pl.ds(me, 1)] = stats_src[pl.ds(d, 1)]

    each_stage(lambda c: c.wait_send(), None)
    for step in range(1, PACKS):
        for model in range(2):
            square_copy(step, model)[0].wait_send()
            full_copy(step, model)[0].wait_send()
    for t in range(3):
        ref = thirds[t].at[pl.ds(0, 63), pl.ds(0, THIRD_ROWS[t])]
        remote(ref, ref, ring_send.at[t], ring_recv.at[0], ahead[0]).wait_send()

    others = stats_in.at[pl.ds(0, PACKS * PACKS - 1)]
    remote(others, others, stats_send, stats_recv, ahead[0]).wait()
    block = stats_in[...]
    top = jnp.max(block, axis=0)
    total = top + jnp.log(jnp.sum(jnp.exp(block - top[None]), axis=0))
    row = lax.broadcasted_iota(jnp.int32, (4, LANES), 0)
    total_out[...] = jnp.where(row < 2, total, jnp.sum(block, axis=0))


def finish(total, doc_ids, token_out, score_out):
    d = lax.axis_index("dom")
    token = total[2:3, :] - total[1:2, :] + total[0:1, :]
    own_docs = doc_ids[pl.ds(d, 1), :]
    token = jnp.where(own_docs >= 0, token, 0.0)
    token_out[...] = token
    row = lax.broadcasted_iota(jnp.int32, (DOC_PACK, LANES), 0)
    col = lax.broadcasted_iota(jnp.int32, (DOC_PACK, LANES), 1)
    member = (own_docs - d * DOC_PACK) == row
    doc_sum = jnp.sum(jnp.where(member, token, 0.0), axis=1, keepdims=True)
    doc_count = jnp.sum(jnp.where(member, 1.0, 0.0), axis=1, keepdims=True)
    score = jnp.sum(jnp.where(row == col, doc_sum / doc_count, 0.0), axis=0, keepdims=True)
    score_out[...] = score[:, :DOC_PACK]


def per_device(gen_hidden, gen_gain, gen_head, dom_hidden, dom_gain, dom_head, targets, doc_ids):
    anywhere = pl.BlockSpec(memory_space=pl.ANY)
    dma = pltpu.SemaphoreType.DMA
    slots = pltpu.VMEM((2 * BLOCKS, THIRD_PAD, LANES), BF16)
    docs = doc_ids.reshape(PACKS, LANES)
    total = pl.pallas_call(
        kernel,
        out_shape=jax.ShapeDtypeStruct((4, LANES), F32),
        in_specs=[anywhere] * 8,
        out_specs=pl.BlockSpec(memory_space=pltpu.VMEM),
        scratch_shapes=[
            pltpu.VMEM((2, BLOCKS, VOCAB_DEV, LANES), BF16),
            slots,
            slots,
            slots,
            pltpu.VMEM((6, VOCAB_DEV, THIRD_PAD), F32),
            pltpu.VMEM((3, THIRD_PAD, PACKS * PACK_ROWS), BF16),
            pltpu.VMEM((PACKS, PACK_ROWS, LANES), BF16),
            pltpu.VMEM((2, PACK_ROWS, 4 * LANES), BF16),
            pltpu.VMEM((2, BLOCKS, LANES), F32),
            pltpu.VMEM((2, PACKS, LANES), jnp.int32),
            pltpu.VMEM((2 * PACKS, 1, LANES), F32),
            pltpu.VMEM((2 * PACKS, 1, LANES), F32),
            pltpu.VMEM((2, 1, LANES), F32),
            pltpu.VMEM((2, 1, LANES), F32),
            pltpu.VMEM((3, PACKS * PACK_ROWS, LANES), BF16),
            pltpu.VMEM((6, THIRD_PAD, LANES), F32),
            pltpu.VMEM((PACKS, 4, LANES), F32),
            pltpu.VMEM((PACKS * PACKS, 4, LANES), F32),
            pltpu.VMEM((3, 8, THIRD_PAD), jnp.int32),
            pltpu.VMEM((32, PACKS * PACK_ROWS), BF16),
            dma((6,)),
            dma((2,)),
            dma((8,)),
            dma((8,)),
            dma,
            dma((16,)),
            dma((16,)),
            dma((16,)),
            dma((16,)),
            dma((3,)),
            dma((192,)),
            dma,
            dma,
        ],
        compiler_params=pltpu.CompilerParams(
            collective_id=0, has_side_effects=True, vmem_limit_bytes=60 * 1024 * 1024
        ),
        cost_estimate=pl.CostEstimate(
            flops=4 * LIVE_ROWS * VOCAB_DEV * WIDTH,
            bytes_accessed=4 * VOCAB_DEV * WIDTH,
            transcendentals=2 * LIVE_ROWS * VOCAB_DEV,
        ),
    )(
        gen_hidden,
        gen_gain.reshape(BLOCKS, LANES),
        gen_head,
        dom_hidden,
        dom_gain.reshape(BLOCKS, LANES),
        dom_head,
        targets.reshape(PACKS, LANES),
        docs,
    )
    token, score = pl.pallas_call(
        finish,
        out_shape=(
            jax.ShapeDtypeStruct((1, PACK_ROWS), F32),
            jax.ShapeDtypeStruct((1, DOC_PACK), F32),
        ),
    )(total, docs)
    return token.reshape(PACK_ROWS), score.reshape(DOC_PACK)


def solution(mesh):
    in_specs = (
        P(("dp", "dom"), "gen"),
        P("dp"),
        P(("dp", "gen", "dom"), None),
        P(("dp", "gen"), "dom"),
        P("dp"),
        P(("dp", "gen", "dom"), None),
        P("dp"),
        P("dp"),
    )
    out_specs = (P(("dp", "dom")), P(("dp", "dom")))
    return jax.shard_map(
        per_device, mesh=mesh, in_specs=in_specs, out_specs=out_specs, check_vma=False
    )
```
